256 devices in a mesh: tm: 32 (over z_hi, y, core), rows: 8 (over z_lo, x).
Axes of the slice: x: 4, y: 4, z: 8 (z_hi: 4, z_lo: 2; z = z_hi * 2 + z_lo), core: 2. Of those that a mesh axis runs over, the one named last changes fastest.
Arguments:
- frames_in: bfloat16 [32, 48, 160, 256], P('tm', 'rows'), may hold values from -6 to 6
- grad_out: bfloat16 [32, 48, 160, 256], P('tm', 'rows'), may hold values from -6 to 6
- conv_weight: bfloat16 [2, 9, 256, 256], replicated, may hold values from -0.125 to 0.125
- attn_weight: bfloat16 [4, 256, 256], replicated, may hold values from -0.375 to 0.375
Outputs:
- input_grad: bfloat16 [32, 48, 160, 256], P('tm', 'rows')
- conv_grad: float32 [2, 9, 256, 256], P(None, None, 'tm')
- attn_grad: float32 [4, 256, 256], P(None, 'tm')
The draws below stay inside these ranges and needn't reach their ends.
All inputs are finite; a program needn't handle non-finite values.
Results may differ from the reference program's by a relative error of at most 0.027.
Values may be sent and summed in bfloat16 or wider, within the bound.
A program may use at most 64 MiB of HBM per device.

```python
import jax
import jax.numpy as jnp
from jax import lax

C = 256
HEADS = 4
W = 160
FRAMES = 32
H = 48


def spiked(result, rng, source, target, shards_of, factor):
    def block_of(dim):
        return (jnp.arange(result.shape[dim]) // (result.shape[dim] // shards_of)).reshape((-1,) + (1,) * (result.ndim - 1 - dim))

    one_side = jax.random.permutation(rng, shards_of)[block_of(target)]
    far = (block_of(target) + shards_of // 2) % shards_of
    return jnp.where((block_of(source) == one_side) | (block_of(source) == far), factor * result, result)


def shard_levels(own_key, dims, split, least, top_value):
    loudness, own = 1.0, jax.random.fold_in(own_key, 6)
    for axis_at, blocks in split:
        heights = jnp.exp(jax.random.uniform(jax.random.fold_in(own, axis_at), (blocks,), jnp.float32, least / len(split), top_value / len(split)))
        loudness = loudness * jnp.repeat(heights, dims[axis_at] // blocks).reshape([-1 if axis == axis_at else 1 for axis in range(len(dims))])
    return loudness


def gaussian(rng, dims, scale, bound, split=(), held_as=jnp.bfloat16):
    factor_of = shard_levels(rng, dims, split, -0.22, 0.18) if split else 1.0
    array = jax.random.normal(rng, dims, jnp.float32) * scale * factor_of
    return jnp.minimum(jnp.maximum(array, -bound), bound).astype(held_as)


def gaussian_with(stream_key, dims, scale, limit, cuts, heavy, kind=jnp.bfloat16):
    array = scale * jax.random.normal(stream_key, dims, jnp.float32)
    if cuts:
        array = array * shard_levels(stream_key, dims, cuts, -0.22, 0.18)
    return jnp.clip(spiked(array, jax.random.fold_in(stream_key, 3), *heavy), -limit, limit).astype(kind)


def setup_inputs(seed: int = 0) -> dict:
    arg_keys = jax.random.split(jax.random.key(seed), 5)
    frames_in = gaussian_with(arg_keys[0], (FRAMES, H, W, C), 1.0, 6.0, ((0, 32), (1, 8)), (0, 3, 32, 2.75))
    grad_out = gaussian(arg_keys[1], (FRAMES, H, W, C), 1.0, 6.0, ((0, 32), (1, 8)))
    conv_weight = gaussian(arg_keys[2], (2, 9, C, C), (9 * C) ** -0.5, 0.125)
    attn_weight = gaussian(arg_keys[3], (4, C, C), C ** -0.5, 0.375)
    return dict(frames_in=frames_in, grad_out=grad_out, conv_weight=conv_weight, attn_weight=attn_weight)


EPSILON = 1e-06

def pad_both(values):
    return jnp.pad(values, ((0, 0), (1, 1), (1, 1), (0, 0)))

def conv_fwd(padded, weight, count):
    width = padded.shape[2] - 2
    total = None
    for row_off in range(3):
        for col_off in range(3):
            window = padded[:, row_off:row_off + count, col_off:col_off + width]
            term = jnp.einsum('frwc,cd->frwd', window, weight[3 * row_off + col_off])
            total = term if total is None else total + term
    return total

def conv_back(padded, weight, count):
    width = padded.shape[2] - 2
    total = None
    for row_off in range(3):
        for col_off in range(3):
            window = padded[:, 2 - row_off:2 - row_off + count, 2 - col_off:2 - col_off + width]
            term = jnp.einsum('frwd,cd->frwc', window, weight[3 * row_off + col_off])
            total = term if total is None else total + term
    return total

def weight_grad(padded, upstream):
    count = upstream.shape[1]
    width = upstream.shape[2]
    pieces = []
    for row_off in range(3):
        for col_off in range(3):
            window = padded[:, row_off:row_off + count, col_off:col_off + width]
            pieces.append(jnp.einsum('frwc,frwd->cd', window, upstream))
    return jnp.stack(pieces)

def silu_slope(pre):
    sig = jax.nn.sigmoid(pre)
    return sig * (1.0 + pre * (1.0 - sig))

def temporal_backward(mixed, upstream, attn_weight):
    frames, pixels, width = mixed.shape
    head_size = width // HEADS
    f32 = jnp.float32
    bf16 = jnp.bfloat16
    mixed_f = mixed.astype(f32)
    norm_scale = lax.rsqrt(lax.optimization_barrier(jnp.mean(mixed_f * mixed_f, axis=-1, keepdims=True)) + EPSILON)
    normed = (mixed_f * norm_scale).astype(bf16).reshape(frames * pixels, width)
    joined = jnp.concatenate([attn_weight[0], attn_weight[1], attn_weight[2]], axis=1)
    projected = jnp.dot(normed, joined, preferred_element_type=f32).astype(bf16)
    shaped = projected.reshape(frames, pixels, 3, HEADS, head_size)
    queries = shaped[:, :, 0].astype(f32)
    keys_all = shaped[:, :, 1].astype(f32)
    values_all = shaped[:, :, 2].astype(f32)
    factor = head_size ** (-0.5)
    scores = jnp.einsum('fqhd,gqhd->qhfg', queries, keys_all) * factor
    expo = jnp.exp(scores)
    probs = expo / lax.optimization_barrier(jnp.sum(expo, axis=-1, keepdims=True))
    probs_low = probs.astype(bf16).astype(f32)
    attended = jnp.einsum('qhfg,gqhd->fqhd', probs_low, values_all).astype(bf16).reshape(frames * pixels, width)
    upstream_flat = upstream.reshape(frames * pixels, width)
    grad_att = lax.dot_general(upstream_flat, attn_weight[3], (((1,), (1,)), ((), ())), preferred_element_type=f32).astype(bf16)
    out_grad = lax.dot_general(attended, upstream_flat, (((0,), (0,)), ((), ())), preferred_element_type=f32)
    grad_heads = grad_att.reshape(frames, pixels, HEADS, head_size).astype(f32)
    grad_probs = jnp.einsum('fqhd,gqhd->qhfg', grad_heads, values_all)
    grad_values = jnp.einsum('qhfg,fqhd->gqhd', probs_low, grad_heads).astype(bf16)
    grad_scores = probs * (grad_probs - lax.optimization_barrier(jnp.sum(probs * grad_probs, axis=-1, keepdims=True)))
    scores_low = (grad_scores * factor).astype(bf16).astype(f32)
    grad_queries = jnp.einsum('qhfg,gqhd->fqhd', scores_low, keys_all).astype(bf16)
    grad_keys = jnp.einsum('qhfg,fqhd->gqhd', scores_low, queries).astype(bf16)
    grad_joined = jnp.concatenate([grad_queries.reshape(frames * pixels, width), grad_keys.reshape(frames * pixels, width), grad_values.reshape(frames * pixels, width)], axis=1)
    grad_normed = lax.dot_general(grad_joined, joined, (((1,), (1,)), ((), ())), preferred_element_type=f32).reshape(frames, pixels, width)
    proj_grad = lax.dot_general(normed, grad_joined, (((0,), (0,)), ((), ())), preferred_element_type=f32)
    inner = lax.optimization_barrier(jnp.mean(grad_normed * mixed_f, axis=-1, keepdims=True))
    grad_mixed = norm_scale * grad_normed - mixed_f * norm_scale * norm_scale * norm_scale * inner
    total_grad = (upstream.astype(f32) + grad_mixed).astype(bf16)
    weights_grad = jnp.stack([proj_grad[:, :width], proj_grad[:, width:2 * width], proj_grad[:, 2 * width:], out_grad])
    return (total_grad, weights_grad)

def reference(frames_in, grad_out, conv_weight, attn_weight):
    frames, height, width, chans = frames_in.shape
    f32 = jnp.float32
    bf16 = jnp.bfloat16
    inputs_f = frames_in.astype(f32)
    kernels = conv_weight.astype(f32)
    hidden_pre = conv_fwd(pad_both(inputs_f), kernels[0], height)
    hidden_act = jax.nn.silu(hidden_pre).astype(bf16)
    act_pad = pad_both(hidden_act.astype(f32))
    branch = conv_fwd(act_pad, kernels[1], height)
    mixed = (inputs_f + branch).astype(bf16)
    grad_flat, attn_sums = temporal_backward(mixed.reshape(frames, height * width, chans), grad_out.reshape(frames, height * width, chans), attn_weight)
    grad_mixed = grad_flat.reshape(frames, height, width, chans).astype(f32)
    act_grad = conv_back(pad_both(grad_mixed), kernels[1], height).astype(bf16)
    second = weight_grad(act_pad, grad_mixed)
    pre_grad = (act_grad.astype(f32) * silu_slope(hidden_pre)).astype(bf16).astype(f32)
    input_grad = (grad_mixed + conv_back(pad_both(pre_grad), kernels[0], height)).astype(bf16)
    first = weight_grad(pad_both(inputs_f), pre_grad)
    scale = float(frames * height * width) ** (-0.5)
    return (input_grad, jnp.stack([first, second]) * scale, attn_sums * scale)
```

```python
import functools

import jax
import jax.numpy as jnp
from jax import lax
from jax.experimental import pallas as pl
from jax.experimental.pallas import tpu as pltpu
from jax.sharding import PartitionSpec as P

HEADS = 4
EPSILON = 1e-06
T, R = 32, 8
NR, W, C = 6, 160, 256
PIX = 32
CHUNKS = NR * W // PIX
EARLY, LATE = 96, 80
F32, BF16 = jnp.float32, jnp.bfloat16
MESH = pl.DeviceIdType.MESH
VMEM_LIMIT = 60 * 1024 * 1024


def barrier(tm, rows, row_peers):
    sem = pltpu.get_barrier_semaphore()

    def tell_tm(s, _):
        pl.semaphore_signal(
            sem, inc=1, device_id={"tm": lax.rem(tm + s, T)}, device_id_type=MESH
        )
        return 0

    lax.fori_loop(1, T, tell_tm, 0)
    for s in row_peers:
        pl.semaphore_signal(
            sem, inc=1, device_id={"rows": lax.rem(rows + s, R)}, device_id_type=MESH
        )
    pl.semaphore_wait(sem, T - 1 + len(row_peers))


def chunk_copy(src, dst, ss, rs, mine, peer, slot):
    return pltpu.make_async_remote_copy(
        src_ref=src.at[peer],
        dst_ref=dst.at[slot],
        send_sem=ss.at[peer],
        recv_sem=rs.at[slot],
        device_id={"tm": peer},
        device_id_type=MESH,
    )


def spread_start(src, dst, ss, rs, tm):
    def go(s, _):
        peer = lax.rem(tm + s, T)
        chunk_copy(src, dst, ss, rs, tm, peer, tm).start()
        return 0

    lax.fori_loop(1, T, go, 0)
    dst[tm] = src[tm]


def spread_wait(src, dst, ss, rs, tm):
    def go(s, _):
        peer = lax.rem(tm + T - s, T)
        copy = chunk_copy(src, dst, ss, rs, tm, peer, peer)
        copy.wait_send()
        copy.wait_recv()
        return 0

    lax.fori_loop(1, T, go, 0)


def row_copy(src, dst, ss, rs, peer):
    return pltpu.make_async_remote_copy(
        src_ref=src,
        dst_ref=dst,
        send_sem=ss,
        recv_sem=rs,
        device_id={"rows": peer},
        device_id_type=MESH,
    )


def shifts(row):
    col = lax.broadcasted_iota(jnp.int32, (W, C), 0)
    before = jnp.where(col == 0, 0.0, pltpu.roll(row, 1, 0))
    after = jnp.where(col == W - 1, 0.0, pltpu.roll(row, W - 1, 0))
    return before, row, after


def fill(src, dst, first, count, forward):
    def go(i, _):
        before, here, after = shifts(src[i].astype(F32))
        parts = (before, here, after) if forward else (after, here, before)
        for b in range(3):
            dst[i, :, b * C : (b + 1) * C] = parts[b].astype(BF16)
        return 0

    lax.fori_loop(first, first + count, go, 0)


def taps(wide, start, count, forward):
    pieces = []
    for a in range(3):
        off = a if forward else 2 - a
        pieces.append(wide[pl.ds(start + off, count)].reshape(count * W, 3 * C))
    return jnp.concatenate(pieces, axis=1)


def forward_kernel(
    x_ref, g_ref, w_ref,
    xe, ae, slope, mt, gt, kt,
    gpad, mpad, xc, ac, hid,
    gs, gr, ms, mr, hs, hr,
):
    tm, rows = lax.axis_index("tm"), lax.axis_index("rows")
    up, down = lax.rem(rows + R - 1, R), lax.rem(rows + 1, R)
    gpad[0:CHUNKS] = g_ref[...]
    gpad[CHUNKS:T] = jnp.zeros((T - CHUNKS, PIX, C), BF16)
    mpad[CHUNKS:T] = jnp.zeros((T - CHUNKS, PIX, C), BF16)
    barrier(tm, rows, (1, R - 1))
    to_up = row_copy(x_ref.at[pl.ds(0, 2)], xe.at[pl.ds(NR + 2, 2)], hs.at[0], hr.at[0], up)
    to_down = row_copy(x_ref.at[pl.ds(NR - 2, 2)], xe.at[pl.ds(0, 2)], hs.at[1], hr.at[1], down)
    to_up.start()
    to_down.start()
    spread_start(gpad, gt, gs, gr, tm)
    xe[2 : NR + 2] = x_ref[...]
    fill(xe, xc, 2, NR, True)
    to_up.wait()
    to_down.wait()

    @pl.when(rows == 0)
    def _():
        xe[0:2] = jnp.zeros((2, W, C), BF16)

    @pl.when(rows == R - 1)
    def _():
        xe[NR + 2 : NR + 4] = jnp.zeros((2, W, C), BF16)

    fill(xe, xc, 0, 2, True)
    fill(xe, xc, NR + 2, 2, True)

    def first(i, _):
        s = i * 2
        hidden = jnp.dot(taps(xc, s, 2, True), w_ref[0], preferred_element_type=F32)
        hidden = hidden.reshape(2, W, C)
        hid[pl.ds(s, 2)] = hidden
        ae[pl.ds(s, 2)] = (hidden * jax.nn.sigmoid(hidden)).astype(BF16)
        return 0

    lax.fori_loop(0, 4, first, 0)

    @pl.when(rows == 0)
    def _():
        ae[0:1] = jnp.zeros((1, W, C), BF16)

    @pl.when(rows == R - 1)
    def _():
        ae[NR + 1 : NR + 2] = jnp.zeros((1, W, C), BF16)

    fill(ae, ac, 0, NR + 2, True)

    def second(i, _):
        s = i * 2
        branch = jnp.dot(taps(ac, s, 2, True), w_ref[1], preferred_element_type=F32)
        mixed = x_ref[pl.ds(s, 2)].astype(F32).reshape(2 * W, C) + branch
        mpad[pl.ds(i * 10, 10)] = mixed.astype(BF16).reshape(10, PIX, C)
        return 0

    lax.fori_loop(0, 3, second, 0)
    spread_start(mpad, mt, ms, mr, tm)

    def turn(i, _):
        for k in range(2):
            at = pl.ds(pl.multiple_of(i * C, C), C)
            kt[k, at, :] = w_ref[k, at, :].astype(F32).T.astype(BF16)
        return 0

    lax.fori_loop(0, 9, turn, 0)

    def slopes(i, _):
        h = hid[i]
        s = jax.nn.sigmoid(h)
        slope[i] = s * (1.0 + h * (1.0 - s))
        return 0

    lax.fori_loop(0, NR + 2, slopes, 0)
    spread_wait(gpad, gt, gs, gr, tm)
    spread_wait(mpad, mt, ms, mr, tm)


def nt(a, b):
    return lax.dot_general(a, b, (((1,), (1,)), ((), ())), preferred_element_type=F32)


def tn(a, b):
    return lax.dot_general(a, b, (((0,), (0,)), ((), ())), preferred_element_type=F32)


def attention_kernel(mt, gt, aw, out, wg, stage, stage_g, mix, gup, normed, scale, qkv, ga, att, gj):
    joined = jnp.concatenate([aw[0], aw[1], aw[2]], axis=1)
    n = T * PIX

    def widen(f, _):
        at = pl.ds(pl.multiple_of(f * PIX, PIX), PIX)
        for half in range(2):
            cols = pl.ds(half * 128, 128)
            stage[half, at, :] = mt[f, :, cols].astype(F32)
            stage_g[half, at, :] = gt[f, :, cols].astype(F32)
        return 0

    lax.fori_loop(0, T, widen, 0)

    def by_pixel(p, _):
        at = pl.ds(pl.multiple_of(p * T, T), T)
        m = jnp.concatenate([stage[h, pl.ds(p, T, stride=PIX), :] for h in range(2)], axis=1)
        g = jnp.concatenate([stage_g[h, pl.ds(p, T, stride=PIX), :] for h in range(2)], axis=1)
        ns = lax.rsqrt(jnp.mean(m * m, axis=-1, keepdims=True) + EPSILON)
        mix[at, :] = m
        scale[at, :] = jnp.broadcast_to(ns, (T, 128))
        normed[at, :] = (m * ns).astype(BF16)
        gup[at, :] = g.astype(BF16)
        return 0

    lax.fori_loop(0, PIX, by_pixel, 0)
    step = 256
    for i in range(n // step):
        at = slice(i * step, (i + 1) * step)
        qkv[at, :] = jnp.dot(normed[at, :], joined, preferred_element_type=F32).astype(BF16)
        ga[at, :] = nt(gup[at, :], aw[3]).astype(BF16)

    factor = 64.0**-0.5
    g = 128
    lane = lax.broadcasted_iota(jnp.int32, (1, C), 1) // 64
    head = [(lane == h).astype(F32).astype(BF16) for h in range(HEADS)]
    blocks = (
        lax.rem(lax.broadcasted_iota(jnp.int32, (HEADS * g, g), 0), g) // T
        == lax.broadcasted_iota(jnp.int32, (HEADS * g, g), 1) // T
    )

    def stack(x):
        return jnp.concatenate([x * head[h] for h in range(HEADS)], axis=0)

    def side(x):
        return jnp.concatenate([x[h * g : (h + 1) * g] for h in range(HEADS)], axis=1)

    def group(i, _):
        at = pl.ds(pl.multiple_of(i * g, g), g)
        q, k, v = qkv[at, 0:C], qkv[at, C : 2 * C], qkv[at, 2 * C : 3 * C]
        a = ga[at, :]
        qs, ks, vs, gas = stack(q), stack(k), stack(v), stack(a)
        expo = jnp.where(blocks, jnp.exp(nt(qs, k) * factor), 0.0)
        probs = expo / jnp.sum(expo, axis=-1, keepdims=True)
        low = probs.astype(BF16)
        att[at, :] = jnp.dot(side(low), vs, preferred_element_type=F32).astype(BF16)
        gp = nt(gas, v)
        gs = probs * (gp - jnp.sum(probs * gp, axis=-1, keepdims=True))
        sl = (gs * factor).astype(BF16)
        gj[at, 0:C] = jnp.dot(side(sl), ks, preferred_element_type=F32).astype(BF16)
        gj[at, C : 2 * C] = tn(sl, qs).astype(BF16)
        gj[at, 2 * C : 3 * C] = tn(low, gas).astype(BF16)
        return 0

    lax.fori_loop(0, n // g, group, 0)
    for i in range(n // step):
        at = slice(i * step, (i + 1) * step)
        gn = nt(gj[at, :], joined)
        m = mix[at, :]
        ns = jnp.concatenate([scale[at, :]] * 2, axis=1)
        inner = jnp.mean(gn * m, axis=-1, keepdims=True)
        total = gup[at, :].astype(F32) + (ns * gn - m * ns * ns * ns * inner)
        for h in range(2):
            stage[h, at, :] = total[:, h * 128 : (h + 1) * 128]

    def by_frame(f, _):
        for h in range(2):
            out[f, :, pl.ds(h * 128, 128)] = stage[h, pl.ds(f, PIX, stride=T), :].astype(BF16)
        return 0

    lax.fori_loop(0, T, by_frame, 0)
    proj = tn(normed[...], gj[...])
    for k in range(3):
        wg[k] = proj[:, k * C : (k + 1) * C]
    wg[3] = tn(att[...], gup[...])


def slab(t):
    z, y, c = t // 8, (t // 2) % 4, t % 2
    return c, y * 4 + z


def pack(dst, row, upper, lower):
    for t in range(T):
        c, k = slab(t)
        both = jnp.concatenate([upper[t * 8 : t * 8 + 8], lower[t * 8 : t * 8 + 8]], axis=0)
        dst[c, k, row : row + 16, :] = both.astype(BF16)


class Reduction:
    def __init__(self, n, packed, r1, a1, r2, a2, r3, a3, r4, ss, rs, tm, rows):
        self.n, self.packed, self.r1, self.a1, self.r2 = n, packed, r1, a1, r2
        self.a2, self.r3, self.a3, self.r4 = a2, r3, a3, r4
        self.ss, self.rs, self.tm, self.rows = ss, rs, tm, rows
        self.core, self.y, self.z = lax.rem(tm, 2), lax.rem(tm // 2, 4), tm // 8

    def copy(self, src, dst, s, dev):
        return pltpu.make_async_remote_copy(
            src_ref=src, dst_ref=dst, send_sem=self.ss.at[s], recv_sem=self.rs.at[s],
            device_id=dev, device_id_type=MESH,
        )

    def core_copy(self):
        return self.copy(
            self.packed.at[1 - self.core], self.r1, 0, {"tm": self.tm + 1 - 2 * self.core}
        )

    def y_copy(self, s):
        y = lax.rem(self.y + s, 4)
        return self.copy(
            self.a1.at[y], self.r2.at[s - 1], s, {"tm": self.z * 8 + y * 2 + self.core}
        )

    def z_copy(self, s):
        z = lax.rem(self.z + s, 4)
        return self.copy(
            self.a2.at[z], self.r3.at[s - 1], 3 + s, {"tm": z * 8 + self.y * 2 + self.core}
        )

    def row_copy(self, s):
        peer = lax.rem(self.rows + s, R)
        return self.copy(self.a3, self.r4.at[s - 1], 6 + s, {"rows": peer})

    def start(self):
        self.core_copy().start()

    def after_core(self):
        self.core_copy().wait()

        def add(k, _):
            y, z = k // 4, lax.rem(k, 4)
            self.a1[y, z] = (
                self.packed[self.core, k].astype(F32) + self.r1[k].astype(F32)
            ).astype(BF16)
            return 0

        lax.fori_loop(0, 16, add, 0)
        for s in (1, 2, 3):
            self.y_copy(s).start()

    def after_y(self):
        for s in (1, 2, 3):
            self.y_copy(s).wait()

        def add(z, _):
            total = self.a1[self.y, z].astype(F32)
            for s in range(3):
                total += self.r2[s, z].astype(F32)
            self.a2[z] = total.astype(BF16)
            return 0

        lax.fori_loop(0, 4, add, 0)
        for s in (1, 2, 3):
            self.z_copy(s).start()

    def after_z(self):
        for s in (1, 2, 3):
            self.z_copy(s).wait()
        total = self.a2[self.z].astype(F32)
        for s in range(3):
            total += self.r3[s].astype(F32)
        self.a3[...] = total.astype(BF16)
        for s in range(1, R):
            self.row_copy(s).start()

    def finish(self):
        for s in range(1, R):
            self.row_copy(s).wait()
        self.r4[R - 1] = self.a3[...]
        total = jnp.zeros((self.n, C), F32)
        for row in range(R):
            slot = lax.rem(self.rows + 2 * R - row - 1, R)
            total += self.r4[slot].astype(F32)
        return total * (float(T * NR * R * W) ** -0.5)


def backward_kernel(
    pt, wg, xe, ae, slope, kt,
    dx, dconv, dattn,
    gm, ge, uc, pre, pc, g1,
    ps, pr, hs, hr,
    *bufs,
):
    tm, rows = lax.axis_index("tm"), lax.axis_index("rows")
    up, down = lax.rem(rows + R - 1, R), lax.rem(rows + 1, R)
    early = Reduction(EARLY, *bufs[:10], tm, rows)
    late = Reduction(LATE, *bufs[10:], tm, rows)
    barrier(tm, rows, tuple(range(1, R)))
    spread_start(pt, gm, ps, pr, tm)
    pack(early.packed, 64, wg[0], wg[1])
    pack(early.packed, 80, wg[2], wg[3])
    spread_wait(pt, gm, ps, pr, tm)
    ge[2 : NR + 2] = gm[0:CHUNKS].reshape(NR, W, C)
    to_up = row_copy(ge.at[pl.ds(2, 2)], ge.at[pl.ds(NR + 2, 2)], hs.at[0], hr.at[0], up)
    to_down = row_copy(ge.at[pl.ds(NR, 2)], ge.at[pl.ds(0, 2)], hs.at[1], hr.at[1], down)
    to_up.start()
    to_down.start()
    fill(ge, uc, 2, NR, False)
    for a in range(3):
        g1[a] = tn(
            ae[a : a + NR].reshape(NR * W, C), uc[2 : NR + 2].reshape(NR * W, 3 * C)
        )

    def one(k):
        return g1[k // 3, :, (k % 3) * C : (k % 3 + 1) * C]

    for k in range(0, 8, 2):
        pack(early.packed, k * 8, one(k), one(k + 1))
    early.start()
    to_up.wait()
    to_down.wait()

    @pl.when(rows == 0)
    def _():
        ge[0:2] = jnp.zeros((2, W, C), BF16)

    @pl.when(rows == R - 1)
    def _():
        ge[NR + 2 : NR + 4] = jnp.zeros((2, W, C), BF16)

    fill(ge, uc, 0, 2, False)
    fill(ge, uc, NR + 2, 2, False)

    def first(i, _):
        s = i * 2
        act_grad = jnp.dot(taps(uc, s, 2, False), kt[1], preferred_element_type=F32)
        act_grad = act_grad.astype(BF16).astype(F32).reshape(2, W, C)
        pre[pl.ds(s, 2)] = (act_grad * slope[pl.ds(s, 2)]).astype(BF16)
        return 0

    lax.fori_loop(0, 4, first, 0)

    @pl.when(rows == 0)
    def _():
        pre[0:1] = jnp.zeros((1, W, C), BF16)

    @pl.when(rows == R - 1)
    def _():
        pre[NR + 1 : NR + 2] = jnp.zeros((1, W, C), BF16)

    early.after_core()
    fill(pre, pc, 0, NR + 2, False)
    last = g1[2, :, 2 * C : 3 * C]
    g0 = []
    for a in range(3):
        g0.append(
            tn(xe[a + 1 : a + 1 + NR].reshape(NR * W, C), pc[1 : NR + 1].reshape(NR * W, 3 * C))
        )

    def zero(k):
        return g0[k // 3][:, (k % 3) * C : (k % 3 + 1) * C]

    for k in range(0, 8, 2):
        pack(late.packed, k * 8, zero(k), zero(k + 1))
    pack(late.packed, 64, zero(8), last)
    late.start()

    def second(i, _):
        s = i * 2
        back = jnp.dot(taps(pc, s, 2, False), kt[0], preferred_element_type=F32)
        here = ge[pl.ds(s + 2, 2)].astype(F32).reshape(2 * W, C)
        dx[pl.ds(s, 2)] = (here + back).astype(BF16).reshape(2, W, C)
        return 0

    lax.fori_loop(0, 3, second, 0)
    early.after_y()
    late.after_core()
    early.after_z()
    late.after_y()
    sums = early.finish()
    dconv[1, 0:8] = sums[0:64].reshape(8, 8, C)
    dattn[...] = sums[64:96].reshape(4, 8, C)
    late.after_z()
    sums = late.finish()
    dconv[0] = sums[0:72].reshape(9, 8, C)
    dconv[1, 8:9] = sums[72:80].reshape(1, 8, C)


def vmem(count):
    return [pl.BlockSpec(memory_space=pltpu.VMEM)] * count


def dma(count):
    return pltpu.SemaphoreType.DMA((count,))


def params(collective_id):
    if collective_id is None:
        return pltpu.CompilerParams(vmem_limit_bytes=VMEM_LIMIT)
    return pltpu.CompilerParams(
        vmem_limit_bytes=VMEM_LIMIT, collective_id=collective_id, has_side_effects=True
    )


def sum_buffers(n):
    return [
        pltpu.VMEM((2, 16, n, C), BF16),
        pltpu.VMEM((16, n, C), BF16),
        pltpu.VMEM((4, 4, n, C), BF16),
        pltpu.VMEM((3, 4, n, C), BF16),
        pltpu.VMEM((4, n, C), BF16),
        pltpu.VMEM((3, n, C), BF16),
        pltpu.VMEM((n, C), BF16),
        pltpu.VMEM((R, n, C), BF16),
        dma(14),
        dma(14),
    ]


def per_device(frames_in, grad_out, conv_weight, attn_weight):
    x = frames_in.reshape(NR, W, C)
    g = grad_out.reshape(CHUNKS, PIX, C)
    w = conv_weight.reshape(2, 9 * C, C)
    spread = jax.ShapeDtypeStruct((T, PIX, C), BF16)
    xe, ae, slope, mt, gt, kt = pl.pallas_call(
        forward_kernel,
        out_shape=[
            jax.ShapeDtypeStruct((NR + 4, W, C), BF16),
            jax.ShapeDtypeStruct((NR + 2, W, C), BF16),
            jax.ShapeDtypeStruct((NR + 2, W, C), F32),
            spread,
            spread,
            jax.ShapeDtypeStruct((2, 9 * C, C), BF16),
        ],
        in_specs=vmem(3),
        out_specs=vmem(6),
        scratch_shapes=[
            pltpu.VMEM((T, PIX, C), BF16),
            pltpu.VMEM((T, PIX, C), BF16),
            pltpu.VMEM((NR + 4, W, 3 * C), BF16),
            pltpu.VMEM((NR + 2, W, 3 * C), BF16),
            pltpu.VMEM((NR + 2, W, C), F32),
            dma(T), dma(T), dma(T), dma(T), dma(2), dma(2),
        ],
        compiler_params=params(1),
        name="forward",
    )(x, g, w)
    n = T * PIX
    pt, wg = pl.pallas_call(
        attention_kernel,
        out_shape=[spread, jax.ShapeDtypeStruct((4, C, C), F32)],
        in_specs=vmem(3),
        out_specs=vmem(2),
        scratch_shapes=[
            pltpu.VMEM((2, n, 128), F32),
            pltpu.VMEM((2, n, 128), F32),
            pltpu.VMEM((n, C), F32),
            pltpu.VMEM((n, C), BF16),
            pltpu.VMEM((n, C), BF16),
            pltpu.VMEM((n, 128), F32),
            pltpu.VMEM((n, 3 * C), BF16),
            pltpu.VMEM((n, C), BF16),
            pltpu.VMEM((n, C), BF16),
            pltpu.VMEM((n, 3 * C), BF16),
        ],
        compiler_params=params(None),
        name="attention",
    )(mt, gt, attn_weight)
    dx, dconv, dattn = pl.pallas_call(
        backward_kernel,
        out_shape=[
            jax.ShapeDtypeStruct((NR, W, C), BF16),
            jax.ShapeDtypeStruct((2, 9, 8, C), F32),
            jax.ShapeDtypeStruct((4, 8, C), F32),
        ],
        in_specs=vmem(6),
        out_specs=vmem(3),
        scratch_shapes=[
            pltpu.VMEM((T, PIX, C), BF16),
            pltpu.VMEM((NR + 4, W, C), BF16),
            pltpu.VMEM((NR + 4, W, 3 * C), BF16),
            pltpu.VMEM((NR + 2, W, C), BF16),
            pltpu.VMEM((NR + 2, W, 3 * C), BF16),
            pltpu.VMEM((3, C, 3 * C), F32),
            dma(T), dma(T), dma(2), dma(2),
            *sum_buffers(EARLY),
            *sum_buffers(LATE),
        ],
        compiler_params=params(2),
        name="backward",
    )(pt, wg, xe, ae, slope, kt)
    return dx.reshape(1, NR, W, C), dconv, dattn


def solution(mesh):
    return jax.shard_map(
        per_device,
        mesh=mesh,
        in_specs=(P("tm", "rows", None, None), P("tm", "rows", None, None), P(), P()),
        out_specs=(P("tm", "rows", None, None), P(None, None, "tm", None), P(None, "tm", None)),
        check_vma=False,
    )
```

```python
import functools

import jax
import jax.numpy as jnp
from jax import lax
from jax.experimental import pallas as pl
from jax.experimental.pallas import tpu as pltpu
from jax.sharding import PartitionSpec as P

HEADS = 4
EPSILON = 1e-06
T, R = 32, 8
NR, W, C = 6, 160, 256
PIX = 16
UNROLL = 2
EARLY, LATE = 96, 80
F32, BF16 = jnp.float32, jnp.bfloat16
MESH = pl.DeviceIdType.MESH
VMEM_LIMIT = 60 * 1024 * 1024


def signal(sem, device):
    pl.semaphore_signal(sem, inc=1, device_id=device, device_id_type=MESH)


def barrier(tm, rows):
    sem = pltpu.get_barrier_semaphore()

    def tell_tm(s, _):
        signal(sem, {"tm": lax.rem(tm + s, T)})
        return 0

    lax.fori_loop(1, T, tell_tm, 0)
    for s in range(1, R):
        signal(sem, {"rows": lax.rem(rows + s, R)})
    for s in (8, 16, 24):
        signal(sem, {"tm": lax.rem(tm + s, T), "rows": lax.rem(rows + 4, R)})
    pl.semaphore_wait(sem, T - 1 + R - 1 + 3)


def remote(src, dst, ss, rs, device):
    return pltpu.make_async_remote_copy(
        src_ref=src,
        dst_ref=dst,
        send_sem=ss,
        recv_sem=rs,
        device_id=device,
        device_id_type=MESH,
    )


def chunk_copy(bufs, half, peer, slot):
    src, dst, ss, rs = bufs
    return remote(
        src.at[half, peer], dst.at[half, slot], ss.at[half, peer], rs.at[half, slot], {"tm": peer}
    )


def spread_start(bufs, half, tm):
    def go(s, _):
        chunk_copy(bufs, half, lax.rem(tm + s, T), tm).start()
        return 0

    lax.fori_loop(1, T, go, 0)
    bufs[1][half, tm] = bufs[0][half, tm]


def spread_wait(bufs, half, tm):
    def go(s, _):
        peer = lax.rem(tm + T - s, T)
        copy = chunk_copy(bufs, half, peer, peer)
        copy.wait_send()
        copy.wait_recv()
        return 0

    lax.fori_loop(1, T, go, 0)


def shifts(row):
    col = lax.broadcasted_iota(jnp.int32, (W, C), 0)
    before = jnp.where(col == 0, 0.0, pltpu.roll(row, 1, 0))
    after = jnp.where(col == W - 1, 0.0, pltpu.roll(row, W - 1, 0))
    return before, row, after


def fill(src, dst, first, count, forward):
    def go(i, _):
        before, here, after = shifts(src[i].astype(F32))
        parts = (before, here, after) if forward else (after, here, before)
        for b in range(3):
            dst[i, :, b * C : (b + 1) * C] = parts[b].astype(BF16)
        return 0

    lax.fori_loop(first, first + count, go, 0)


def taps(wide, start, count, forward):
    pieces = []
    for a in range(3):
        off = a if forward else 2 - a
        pieces.append(wide[start + off : start + off + count].reshape(count * W, 3 * C))
    return jnp.concatenate(pieces, axis=1)


def conv(wide, runs, weight, forward):
    lhs = [taps(wide, start, count, forward) for start, count in runs]
    lhs = lhs[0] if len(lhs) == 1 else jnp.concatenate(lhs, axis=0)
    out = jnp.dot(lhs, weight, preferred_element_type=F32)
    return out.reshape(out.shape[0] // W, W, C)


def nt(a, b):
    return lax.dot_general(a, b, (((1,), (1,)), ((), ())), preferred_element_type=F32)


def tn(a, b):
    return lax.dot_general(a, b, (((0,), (0,)), ((), ())), preferred_element_type=F32)


def attend(half, mt, gt, pt, aw, joined, work, unroll):
    stage, stage_g, mix, scale, qkv, ga, gup, normed, att, gj = work
    n = T * PIX
    base = half * n

    def widen(f, _):
        at = pl.ds(pl.multiple_of(f * PIX, PIX), PIX)
        for h in range(2):
            cols = pl.ds(h * 128, 128)
            stage[h, at, :] = mt[half, f, :, cols].astype(F32)
            stage_g[h, at, :] = gt[half, f, :, cols].astype(F32)
        return 0

    lax.fori_loop(0, T, widen, 0, unroll=4)

    def by_pixel(p, _):
        at = pl.ds(pl.multiple_of(p * T, T), T)
        to = pl.ds(pl.multiple_of(base + p * T, T), T)
        m = jnp.concatenate([stage[h, pl.ds(p, T, stride=PIX), :] for h in range(2)], axis=1)
        g = jnp.concatenate([stage_g[h, pl.ds(p, T, stride=PIX), :] for h in range(2)], axis=1)
        ns = lax.rsqrt(jnp.mean(m * m, axis=-1, keepdims=True) + EPSILON)
        mix[at, :] = m
        scale[at, :] = jnp.broadcast_to(ns, (T, 128))
        normed[to, :] = (m * ns).astype(BF16)
        gup[to, :] = g.astype(BF16)
        return 0

    lax.fori_loop(0, PIX, by_pixel, 0, unroll=4)
    every = pl.ds(base, n)
    qkv[...] = jnp.dot(normed[every, :], joined[...], preferred_element_type=F32).astype(BF16)
    ga[...] = nt(gup[every, :], aw[3]).astype(BF16)

    factor = 64.0**-0.5
    g = 128
    lane = lax.broadcasted_iota(jnp.int32, (1, C), 1) // 64
    head = [(lane == h).astype(F32).astype(BF16) for h in range(HEADS)]
    blocks = (
        lax.rem(lax.broadcasted_iota(jnp.int32, (HEADS * g, g), 0), g) // T
        == lax.broadcasted_iota(jnp.int32, (HEADS * g, g), 1) // T
    )

    def stack(x):
        return jnp.concatenate([x * head[h] for h in range(HEADS)], axis=0)

    def side(x):
        return jnp.concatenate([x[h * g : (h + 1) * g] for h in range(HEADS)], axis=1)

    def group(i, _):
        at = pl.ds(pl.multiple_of(i * g, g), g)
        to = pl.ds(pl.multiple_of(base + i * g, g), g)
        q, k, v = qkv[at, 0:C], qkv[at, C : 2 * C], qkv[at, 2 * C : 3 * C]
        qs, ks, vs, gas = stack(q), stack(k), stack(v), stack(ga[at, :])
        expo = jnp.where(blocks, jnp.exp(nt(qs, k) * factor), 0.0)
        probs = expo / jnp.sum(expo, axis=-1, keepdims=True)
        low = probs.astype(BF16)
        att[to, :] = jnp.dot(side(low), vs, preferred_element_type=F32).astype(BF16)
        gp = nt(gas, v)
        gs = probs * (gp - jnp.sum(probs * gp, axis=-1, keepdims=True))
        sl = (gs * factor).astype(BF16)
        gj[to, 0:C] = jnp.dot(side(sl), ks, preferred_element_type=F32).astype(BF16)
        gj[to, C : 2 * C] = tn(sl, qs).astype(BF16)
        gj[to, 2 * C : 3 * C] = tn(low, gas).astype(BF16)
        return 0

    lax.fori_loop(0, n // g, group, 0, unroll=unroll)
    step = 256
    for i in range(n // step):
        at = slice(i * step, (i + 1) * step)
        to = slice(base + i * step, base + (i + 1) * step)
        gn = nt(gj[to, :], joined[...])
        m = mix[at, :]
        ns = jnp.concatenate([scale[at, :]] * 2, axis=1)
        inner = jnp.mean(gn * m, axis=-1, keepdims=True)
        total = gup[to, :].astype(F32) + (ns * gn - m * ns * ns * ns * inner)
        for h in range(2):
            stage[h, at, :] = total[:, h * 128 : (h + 1) * 128]

    def by_frame(f, _):
        for h in range(2):
            pt[half, f, :, pl.ds(h * 128, 128)] = stage[h, pl.ds(f, PIX, stride=T), :].astype(BF16)
        return 0

    lax.fori_loop(0, T, by_frame, 0, unroll=4)


def attend_buffers():
    n = T * PIX
    return [
        pltpu.VMEM((2, n, 128), F32),
        pltpu.VMEM((2, n, 128), F32),
        pltpu.VMEM((n, C), F32),
        pltpu.VMEM((n, 128), F32),
        pltpu.VMEM((n, 3 * C), BF16),
        pltpu.VMEM((n, C), BF16),
        pltpu.VMEM((2 * n, C), BF16),
        pltpu.VMEM((2 * n, C), BF16),
        pltpu.VMEM((2 * n, C), BF16),
        pltpu.VMEM((2 * n, 3 * C), BF16),
    ]


class Reduction:
    count = 13

    @staticmethod
    def buffers(n, nx):
        ny = n - nx
        shapes = [
            (2, 4, 4, nx), (2, 4, 4, ny),
            (4, 4, nx), (4, 4, ny),
            (4, 4, nx), (4, 4, ny),
            (3, 4, nx), (3, 4, ny),
            (3, nx), (3, ny),
            (n,),
            (8, n),
            (n,),
        ]
        return [pltpu.VMEM(s + (C,), BF16) for s in shapes] + [dma(30), dma(30)]

    def __init__(self, n, nx, bufs, tm, rows):
        self.n, self.nx, self.cut = n, nx, 48
        self.px, self.py, self.rx1, self.ry1, self.ax1, self.ay1 = bufs[0:6]
        self.rx2, self.ry2, self.rx3, self.ry3, self.a3, self.r4, self.out = bufs[6:13]
        self.ss, self.rs = bufs[13:15]
        self.core, self.y, self.z_hi = lax.rem(tm, 2), lax.rem(tm // 2, 4), tm // 8
        self.x, self.z_lo = lax.rem(rows, 4), rows // 4
        self.tm, self.rows = tm, rows

    def copy(self, src, dst, s, r, device):
        return remote(src, dst, self.ss.at[s], self.rs.at[r], device)

    def pack(self, row, upper, lower):
        for t in range(T):
            z, y, c = t // 8, (t // 2) % 4, t % 2
            both = jnp.concatenate([upper[t * 8 : t * 8 + 8], lower[t * 8 : t * 8 + 8]], axis=0)
            if row < self.nx:
                self.px[c, z, y, row : row + 16, :] = both.astype(BF16)
            else:
                self.py[c, y, z, row - self.nx : row - self.nx + 16, :] = both.astype(BF16)

    def tm_at(self, z_hi, y):
        return {"tm": z_hi * 8 + y * 2 + self.core}

    def row_at(self, z_lo, x):
        return {"rows": z_lo * 4 + x}

    def first(self):
        other = {"tm": self.tm + 1 - 2 * self.core}
        return (
            self.copy(self.px.at[1 - self.core], self.rx1, 0, 0, other),
            self.copy(self.py.at[1 - self.core], self.ry1, 1, 1, other),
        )

    def second(self):
        copies = []
        for s in (1, 2, 3):
            x, y = lax.rem(self.x + s, 4), lax.rem(self.y + s, 4)
            copies.append(
                self.copy(
                    self.ax1.at[x], self.rx2.at[s - 1], 1 + s, 1 + s, self.row_at(self.z_lo, x)
                )
            )
            copies.append(
                self.copy(
                    self.ay1.at[y], self.ry2.at[s - 1], 4 + s, 4 + s, self.tm_at(self.z_hi, y)
                )
            )
        return copies

    def third(self):
        copies = []
        for s in (1, 2, 3):
            x, y = lax.rem(self.x + s, 4), lax.rem(self.y + s, 4)
            copies.append(
                self.copy(
                    self.ax1.at[self.x, y],
                    self.rx3.at[s - 1], 7 + s, 7 + s, self.tm_at(self.z_hi, y),
                )
            )
            copies.append(
                self.copy(
                    self.ay1.at[self.y, x],
                    self.ry3.at[s - 1], 10 + s, 10 + s, self.row_at(self.z_lo, x),
                )
            )
        return copies

    def piece(self, k):
        return pl.ds(0, self.cut) if k == 0 else pl.ds(self.cut, self.n - self.cut)

    def fourth(self, k):
        z = self.z_hi * 2 + self.z_lo
        at = self.piece(k)
        device = {"tm": self.x * 8 + self.y * 2 + self.core, "rows": k * 4 + self.x}
        return self.copy(self.a3.at[at], self.r4.at[z, at], 14 + k, 14 + z, device)

    def fourth_in(self, k, z):
        at = self.piece(k)
        device = {"tm": self.tm, "rows": self.rows}
        return self.copy(self.a3.at[at], self.r4.at[z, at], 14 + k, 14 + z, device)

    def fifth(self, k, s):
        at = self.piece(k)
        peer = lax.rem(self.rows + s, R)
        return self.copy(self.out.at[at], self.out.at[at], 21 + s, 22 + k, {"rows": peer})

    def holds(self, k):
        return jnp.logical_and(self.z_hi == self.x, self.z_lo == k)

    def away(self, k):
        return jnp.logical_not(self.holds(k))

    def start(self):
        for copy in self.first():
            copy.start()

    def after_core(self):
        for copy in self.first():
            copy.wait()

        def add(k, _):
            i, j = k // 4, lax.rem(k, 4)
            for p, r, a in ((self.px, self.rx1, self.ax1), (self.py, self.ry1, self.ay1)):
                a[i, j] = (p[self.core, i, j].astype(F32) + r[i, j].astype(F32)).astype(BF16)
            return 0

        lax.fori_loop(0, 16, add, 0)
        for copy in self.second():
            copy.start()

    def after_second(self):
        for copy in self.second():
            copy.wait()

        def add(j, _):
            for a, r, me in ((self.ax1, self.rx2, self.x), (self.ay1, self.ry2, self.y)):
                total = a[me, j].astype(F32)
                for s in range(3):
                    total += r[s, j].astype(F32)
                a[me, j] = total.astype(BF16)
            return 0

        lax.fori_loop(0, 4, add, 0)
        for copy in self.third():
            copy.start()

    def after_third(self):
        for copy in self.third():
            copy.wait()
        for a, r, i, j, at in (
            (self.ax1, self.rx3, self.x, self.y, pl.ds(0, self.nx)),
            (self.ay1, self.ry3, self.y, self.x, pl.ds(self.nx, self.n - self.nx)),
        ):
            total = a[i, j].astype(F32)
            for s in range(3):
                total += r[s].astype(F32)
            self.a3[at, :] = total.astype(BF16)
        for k in range(2):

            @pl.when(self.away(k))
            def _():
                self.fourth(k).start()

    def after_fourth(self):
        for k in range(2):

            @pl.when(self.away(k))
            def _():
                self.fourth(k).wait_send()

            @pl.when(self.holds(k))
            def _():
                at = self.piece(k)
                mine = self.z_hi * 2 + k

                def arrived(s, _):
                    self.fourth_in(k, lax.rem(mine + s, 8)).wait_recv()
                    return 0

                lax.fori_loop(1, 8, arrived, 0)
                self.r4[mine, at, :] = self.a3[at, :]
                total = self.r4[0, at, :].astype(F32)
                for z in range(1, 8):
                    total += self.r4[z, at, :].astype(F32)
                self.out[at, :] = total.astype(BF16)
                for s in range(1, R):
                    self.fifth(k, s).start()

    def finish(self):
        for k in range(2):

            @pl.when(self.holds(k))
            def _():
                for s in range(1, R):
                    self.fifth(k, s).wait_send()

            @pl.when(self.away(k))
            def _():
                self.fifth(k, 1).wait_recv()

        return self.out[...].astype(F32) * (float(T * NR * R * W) ** -0.5)


def zero_at(ref, where, condition):
    @pl.when(condition)
    def _():
        ref[where] = jnp.zeros(ref[where].shape, ref.dtype)


def block_kernel(
    x_ref, g_ref, w_ref, aw,
    dx, dconv, dattn,
    xe, ae, hid, kt, joined, gpad, gt, mpad, mt, pt, gm,
    xc, ac, ge, uc, pre, pc, g1,
    gs, gr, ms, mr, ps, pr, hs, hr, ks, kr,
    *bufs,
):
    tm, rows = lax.axis_index("tm"), lax.axis_index("rows")
    up = {"rows": lax.rem(rows + R - 1, R)}
    down = {"rows": lax.rem(rows + 1, R)}
    top, bottom = rows == 0, rows == R - 1
    work, bufs = bufs[:10], bufs[10:]
    early = Reduction(EARLY, 48, bufs[:15], tm, rows)
    late = Reduction(LATE, 48, bufs[15:], tm, rows)
    g_bufs, m_bufs, p_bufs = (gpad, gt, gs, gr), (mpad, mt, ms, mr), (pt, gm, ps, pr)

    gpad[0, 0:10] = g_ref[0:1].reshape(10, PIX, C)
    gpad[0, 10:30] = g_ref[4:6].reshape(20, PIX, C)
    gpad[1, 0:30] = g_ref[1:4].reshape(30, PIX, C)
    for half in range(2):
        gpad[half, 30:32] = jnp.zeros((2, PIX, C), BF16)
        mpad[half, 30:32] = jnp.zeros((2, PIX, C), BF16)
    barrier(tm, rows)
    to_up = remote(x_ref.at[pl.ds(0, 2)], xe.at[pl.ds(NR + 2, 2)], hs.at[0], hr.at[0], up)
    to_down = remote(x_ref.at[pl.ds(NR - 2, 2)], xe.at[pl.ds(0, 2)], hs.at[1], hr.at[1], down)
    to_up.start()
    to_down.start()
    spread_start(g_bufs, 0, tm)
    xe[2 : NR + 2] = x_ref[...]
    fill(xe, xc, 2, NR, True)

    def keep(first, hidden):
        hid[first : first + hidden.shape[0]] = hidden
        ae[first : first + hidden.shape[0]] = (hidden * jax.nn.sigmoid(hidden)).astype(BF16)

    keep(2, conv(xc, ((2, 4),), w_ref[0], True))
    spread_start(g_bufs, 1, tm)
    to_up.wait()
    to_down.wait()
    zero_at(xe, slice(0, 2), top)
    zero_at(xe, slice(NR + 2, NR + 4), bottom)
    fill(xe, xc, 0, 2, True)
    fill(xe, xc, NR + 2, 2, True)
    ends = conv(xc, ((0, 2), (6, 2)), w_ref[0], True)
    keep(0, ends[0:2])
    keep(6, ends[2:4])
    zero_at(ae, slice(0, 1), top)
    zero_at(ae, slice(NR + 1, NR + 2), bottom)
    fill(ae, ac, 0, NR + 2, True)
    branch = conv(ac, ((0, 1), (4, 2)), w_ref[1], True)
    mixed = jnp.concatenate([x_ref[0:1], x_ref[4:6]], axis=0).astype(F32) + branch
    mpad[0, 0:30] = mixed.astype(BF16).reshape(30, PIX, C)
    spread_start(m_bufs, 0, tm)
    mixed = x_ref[1:4].astype(F32) + conv(ac, ((1, 3),), w_ref[1], True)
    mpad[1, 0:30] = mixed.astype(BF16).reshape(30, PIX, C)
    spread_start(m_bufs, 1, tm)
    joined[...] = jnp.concatenate([aw[0], aw[1], aw[2]], axis=1)

    def turn(i, _):
        for k in range(2):
            at = pl.ds(pl.multiple_of(i * C, C), C)
            kt[k, at, :] = w_ref[k, at, :].astype(F32).T.astype(BF16)
        return 0

    lax.fori_loop(0, 9, turn, 0)

    def slopes(i, _):
        h = hid[i]
        s = jax.nn.sigmoid(h)
        hid[i] = s * (1.0 + h * (1.0 - s))
        return 0

    lax.fori_loop(0, NR + 2, slopes, 0)
    for half in range(2):
        spread_wait(g_bufs, half, tm)
        spread_wait(m_bufs, half, tm)
        attend(half, mt, gt, pt, aw, joined, work, UNROLL)
        spread_start(p_bufs, half, tm)

    gup, normed, att, gj = work[6:10]
    proj = tn(normed[...], gj[...])
    early.pack(64, proj[:, 0:C], proj[:, C : 2 * C])
    early.pack(80, proj[:, 2 * C : 3 * C], tn(att[...], gup[...]))

    spread_wait(p_bufs, 0, tm)
    ge[2:3] = gm[0, 0:10].reshape(1, W, C)
    ge[6:8] = gm[0, 10:30].reshape(2, W, C)
    near_up = remote(ge.at[2], ge.at[NR + 2], ks.at[0], kr.at[0], up)
    near_down = remote(ge.at[NR + 1], ge.at[1], ks.at[1], kr.at[1], down)
    near_up.start()
    near_down.start()
    fill(ge, uc, 2, 1, False)
    fill(ge, uc, 6, 2, False)

    def stacked(ref, runs):
        return jnp.concatenate([ref[s : s + n].reshape(n * W, ref.shape[2]) for s, n in runs], axis=0)

    for a in range(3):
        g1[a] = tn(stacked(ae, ((a, 1), (a + 4, 2))), stacked(uc, ((2, 1), (6, 2))))
    spread_wait(p_bufs, 1, tm)
    ge[3:6] = gm[1, 0:30].reshape(3, W, C)
    far_up = remote(ge.at[3], ge.at[NR + 3], ks.at[2], kr.at[2], up)
    far_down = remote(ge.at[NR], ge.at[0], ks.at[3], kr.at[3], down)
    far_up.start()
    far_down.start()
    fill(ge, uc, 3, 3, False)
    for a in range(3):
        g1[a] += tn(stacked(ae, ((a + 1, 3),)), stacked(uc, ((3, 3),)))

    def one(k):
        return g1[k // 3, :, (k % 3) * C : (k % 3 + 1) * C]

    for k in range(0, 8, 2):
        early.pack(k * 8, one(k), one(k + 1))
    early.start()

    def back(first, act_grad):
        at = slice(first, first + act_grad.shape[0])
        pre[at] = (act_grad.astype(BF16).astype(F32) * hid[at]).astype(BF16)

    near_up.wait()
    near_down.wait()
    zero_at(ge, slice(1, 2), top)
    zero_at(ge, slice(NR + 2, NR + 3), bottom)
    fill(ge, uc, 1, 1, False)
    fill(ge, uc, NR + 2, 1, False)
    back(1, conv(uc, ((1, 6),), kt[1], False))
    early.after_core()
    fill(pre, pc, 1, NR, False)
    g0 = [
        tn(xe[a + 1 : a + 1 + NR].reshape(NR * W, C), pc[1 : NR + 1].reshape(NR * W, 3 * C))
        for a in range(3)
    ]

    def zero(k):
        return g0[k // 3][:, (k % 3) * C : (k % 3 + 1) * C]

    for k in range(0, 8, 2):
        late.pack(k * 8, zero(k), zero(k + 1))
    late.pack(64, zero(8), one(8))
    late.start()
    early.after_second()
    far_up.wait()
    far_down.wait()
    zero_at(ge, slice(0, 1), top)
    zero_at(ge, slice(NR + 3, NR + 4), bottom)
    fill(ge, uc, 0, 1, False)
    fill(ge, uc, NR + 3, 1, False)
    ends = conv(uc, ((0, 1), (7, 1)), kt[1], False)
    back(0, ends[0:1])
    back(7, ends[1:2])
    zero_at(pre, slice(0, 1), top)
    zero_at(pre, slice(NR + 1, NR + 2), bottom)
    late.after_core()
    early.after_third()
    fill(pre, pc, 0, 1, False)
    fill(pre, pc, NR + 1, 1, False)
    dx[0:3] = (ge[2:5].astype(F32) + conv(pc, ((0, 3),), kt[0], False)).astype(BF16)
    late.after_second()
    dx[3:6] = (ge[5:8].astype(F32) + conv(pc, ((3, 3),), kt[0], False)).astype(BF16)
    early.after_fourth()
    late.after_third()
    sums = early.finish()
    dconv[1, 0:8] = sums[0:64].reshape(8, 8, C)
    dattn[...] = sums[64:96].reshape(4, 8, C)
    late.after_fourth()
    sums = late.finish()
    dconv[0] = sums[0:72].reshape(9, 8, C)
    dconv[1, 8:9] = sums[72:80].reshape(1, 8, C)


def pass_kernel(a, b, c, x, y, z):
    x[...] = a[...]
    y[...] = b[...]
    z[...] = c[...]


def vmem(count):
    return [pl.BlockSpec(memory_space=pltpu.VMEM)] * count


def dma(*shape):
    return pltpu.SemaphoreType.DMA(shape)


def params(collective_id=None):
    if collective_id is None:
        return pltpu.CompilerParams(vmem_limit_bytes=VMEM_LIMIT)
    return pltpu.CompilerParams(
        vmem_limit_bytes=VMEM_LIMIT, collective_id=collective_id, has_side_effects=True
    )


def per_device(frames_in, grad_out, conv_weight, attn_weight):
    x = frames_in.reshape(NR, W, C)
    g = grad_out.reshape(NR, W, C)
    w = conv_weight.reshape(2, 9 * C, C)
    spread = pltpu.VMEM((2, T, PIX, C), BF16)
    shapes = [
        jax.ShapeDtypeStruct((NR, W, C), BF16),
        jax.ShapeDtypeStruct((2, 9, 8, C), F32),
        jax.ShapeDtypeStruct((4, 8, C), F32),
    ]
    outs = pl.pallas_call(
        block_kernel,
        out_shape=shapes,
        in_specs=vmem(4),
        out_specs=vmem(3),
        scratch_shapes=[
            pltpu.VMEM((NR + 4, W, C), BF16),
            pltpu.VMEM((NR + 2, W, C), BF16),
            pltpu.VMEM((NR + 2, W, C), F32),
            pltpu.VMEM((2, 9 * C, C), BF16),
            pltpu.VMEM((C, 3 * C), BF16),
            *[spread] * 6,
            pltpu.VMEM((NR + 4, W, 3 * C), BF16),
            pltpu.VMEM((NR + 2, W, 3 * C), BF16),
            pltpu.VMEM((NR + 4, W, C), BF16),
            pltpu.VMEM((NR + 4, W, 3 * C), BF16),
            pltpu.VMEM((NR + 2, W, C), BF16),
            pltpu.VMEM((NR + 2, W, 3 * C), BF16),
            pltpu.VMEM((3, C, 3 * C), F32),
            *[dma(2, T)] * 6,
            dma(2), dma(2), dma(4), dma(4),
            *attend_buffers(),
            *Reduction.buffers(EARLY, 48),
            *Reduction.buffers(LATE, 48),
        ],
        compiler_params=params(1),
        name="block",
    )(x, g, w, attn_weight)
    dx, dconv, dattn = pl.pallas_call(
        pass_kernel,
        out_shape=shapes,
        in_specs=vmem(3),
        out_specs=vmem(3),
        compiler_params=params(),
        name="hand_on",
    )(*outs)
    return dx.reshape(1, NR, W, C), dconv, dattn


def solution(mesh):
    return jax.shard_map(
        per_device,
        mesh=mesh,
        in_specs=(P("tm", "rows", None, None), P("tm", "rows", None, None), P(), P()),
        out_specs=(P("tm", "rows", None, None), P(None, None, "tm", None), P(None, "tm", None)),
        check_vma=False,
    )
```

```python
import functools

import jax
import jax.numpy as jnp
from jax import lax
from jax.experimental import pallas as pl
from jax.experimental.pallas import tpu as pltpu
from jax.sharding import PartitionSpec as P

HEADS = 4
EPSILON = 1e-06
T, R = 32, 8
NR, W, C = 6, 160, 256
PIX = 16
UNROLL = 4
F32, BF16 = jnp.float32, jnp.bfloat16
MESH = pl.DeviceIdType.MESH
VMEM_LIMIT = 60 * 1024 * 1024


def signal(sem, device):
    pl.semaphore_signal(sem, inc=1, device_id=device, device_id_type=MESH)


def barrier(tm, rows):
    sem = pltpu.get_barrier_semaphore()

    def tell_tm(s, _):
        signal(sem, {"tm": lax.rem(tm + s, T)})
        return 0

    lax.fori_loop(1, T, tell_tm, 0)
    for s in range(1, R):
        signal(sem, {"rows": lax.rem(rows + s, R)})
    for s in (8, 16, 24):
        signal(sem, {"tm": lax.rem(tm + s, T), "rows": lax.rem(rows + 4, R)})
    pl.semaphore_wait(sem, T - 1 + R - 1 + 3)


def remote(src, dst, ss, rs, device):
    return pltpu.make_async_remote_copy(
        src_ref=src,
        dst_ref=dst,
        send_sem=ss,
        recv_sem=rs,
        device_id=device,
        device_id_type=MESH,
    )


def spread_start(bufs, half, tm):
    src, dst, ss, rs = bufs

    def go(s, _):
        peer = lax.rem(tm + s, T)
        remote(
            src.at[half, peer], dst.at[half, tm], ss.at[half], rs.at[half], {"tm": peer}
        ).start()
        return 0

    lax.fori_loop(1, T, go, 0)
    dst[half, tm] = src[half, tm]


def spread_wait(bufs, half, tm):
    src, dst, ss, rs = bufs
    every = pl.ds(0, T - 1)
    copy = remote(
        src.at[half, every], dst.at[half, every], ss.at[half], rs.at[half],
        {"tm": lax.rem(tm + 1, T)},
    )
    copy.wait_send()
    copy.wait_recv()


def shifts(row):
    col = lax.broadcasted_iota(jnp.int32, (W, C), 0)
    before = jnp.where(col == 0, 0.0, pltpu.roll(row, 1, 0))
    after = jnp.where(col == W - 1, 0.0, pltpu.roll(row, W - 1, 0))
    return before, row, after


def fill(src, dst, first, count, forward):
    def go(i, _):
        before, here, after = shifts(src[i].astype(F32))
        parts = (before, here, after) if forward else (after, here, before)
        for b in range(3):
            dst[i, :, b * C : (b + 1) * C] = parts[b].astype(BF16)
        return 0

    lax.fori_loop(first, first + count, go, 0)


def taps(wide, start, count, forward):
    pieces = []
    for a in range(3):
        off = a if forward else 2 - a
        pieces.append(wide[start + off : start + off + count].reshape(count * W, 3 * C))
    return jnp.concatenate(pieces, axis=1)


def conv(wide, runs, weight, forward):
    lhs = [taps(wide, start, count, forward) for start, count in runs]
    lhs = lhs[0] if len(lhs) == 1 else jnp.concatenate(lhs, axis=0)
    out = jnp.dot(lhs, weight, preferred_element_type=F32)
    return out.reshape(out.shape[0] // W, W, C)


def nt(a, b):
    return lax.dot_general(a, b, (((1,), (1,)), ((), ())), preferred_element_type=F32)


def tn(a, b):
    return lax.dot_general(a, b, (((0,), (0,)), ((), ())), preferred_element_type=F32)


def attend(half, mt, gt, pt, aw, joined, work, unroll):
    stage, stage_g, mix, scale, qkv, ga, gup, normed, att, gj = work
    n = T * PIX
    base = half * n

    def widen(f, _):
        at = pl.ds(pl.multiple_of(f * PIX, PIX), PIX)
        for h in range(2):
            cols = pl.ds(h * 128, 128)
            stage[h, at, :] = mt[half, f, :, cols].astype(F32)
            stage_g[h, at, :] = gt[half, f, :, cols].astype(F32)
        return 0

    lax.fori_loop(0, T, widen, 0, unroll=4)

    def by_pixel(p, _):
        at = pl.ds(pl.multiple_of(p * T, T), T)
        to = pl.ds(pl.multiple_of(base + p * T, T), T)
        m = jnp.concatenate([stage[h, pl.ds(p, T, stride=PIX), :] for h in range(2)], axis=1)
        g = jnp.concatenate([stage_g[h, pl.ds(p, T, stride=PIX), :] for h in range(2)], axis=1)
        ns = lax.rsqrt(jnp.mean(m * m, axis=-1, keepdims=True) + EPSILON)
        mix[at, :] = m
        scale[at, :] = jnp.broadcast_to(ns, (T, 128))
        normed[to, :] = (m * ns).astype(BF16)
        gup[to, :] = g.astype(BF16)
        return 0

    lax.fori_loop(0, PIX, by_pixel, 0, unroll=4)
    every = pl.ds(base, n)
    qkv[...] = jnp.dot(normed[every, :], joined[...], preferred_element_type=F32).astype(BF16)
    ga[...] = nt(gup[every, :], aw[3]).astype(BF16)

    factor = 64.0**-0.5
    g = 128
    lane = lax.broadcasted_iota(jnp.int32, (1, C), 1) // 64
    head = [(lane == h).astype(F32).astype(BF16) for h in range(HEADS)]
    blocks = (
        lax.rem(lax.broadcasted_iota(jnp.int32, (HEADS * g, g), 0), g) // T
        == lax.broadcasted_iota(jnp.int32, (HEADS * g, g), 1) // T
    )

    def stack(x):
        return jnp.concatenate([x * head[h] for h in range(HEADS)], axis=0)

    def side(x):
        return jnp.concatenate([x[h * g : (h + 1) * g] for h in range(HEADS)], axis=1)

    def group(i, _):
        at = pl.ds(pl.multiple_of(i * g, g), g)
        to = pl.ds(pl.multiple_of(base + i * g, g), g)
        q, k, v = qkv[at, 0:C], qkv[at, C : 2 * C], qkv[at, 2 * C : 3 * C]
        qs, ks, vs, gas = stack(q), stack(k), stack(v), stack(ga[at, :])
        expo = jnp.where(blocks, jnp.exp(nt(qs, k) * factor), 0.0)
        probs = expo / jnp.sum(expo, axis=-1, keepdims=True)
        low = probs.astype(BF16)
        att[to, :] = jnp.dot(side(low), vs, preferred_element_type=F32).astype(BF16)
        gp = nt(gas, v)
        gs = probs * (gp - jnp.sum(probs * gp, axis=-1, keepdims=True))
        sl = (gs * factor).astype(BF16)
        gj[to, 0:C] = jnp.dot(side(sl), ks, preferred_element_type=F32).astype(BF16)
        gj[to, C : 2 * C] = tn(sl, qs).astype(BF16)
        gj[to, 2 * C : 3 * C] = tn(low, gas).astype(BF16)
        return 0

    lax.fori_loop(0, n // g, group, 0, unroll=unroll)
    step = 256
    for i in range(n // step):
        at = slice(i * step, (i + 1) * step)
        to = slice(base + i * step, base + (i + 1) * step)
        gn = nt(gj[to, :], joined[...])
        m = mix[at, :]
        ns = jnp.concatenate([scale[at, :]] * 2, axis=1)
        inner = jnp.mean(gn * m, axis=-1, keepdims=True)
        total = gup[to, :].astype(F32) + (ns * gn - m * ns * ns * ns * inner)
        for h in range(2):
            stage[h, at, :] = total[:, h * 128 : (h + 1) * 128]

    def by_frame(f, _):
        for h in range(2):
            pt[half, f, :, pl.ds(h * 128, 128)] = stage[h, pl.ds(f, PIX, stride=T), :].astype(BF16)
        return 0

    lax.fori_loop(0, T, by_frame, 0, unroll=4)


def attend_buffers():
    n = T * PIX
    return [
        pltpu.VMEM((2, n, 128), F32),
        pltpu.VMEM((2, n, 128), F32),
        pltpu.VMEM((n, C), F32),
        pltpu.VMEM((n, 128), F32),
        pltpu.VMEM((n, 3 * C), BF16),
        pltpu.VMEM((n, C), BF16),
        pltpu.VMEM((2 * n, C), BF16),
        pltpu.VMEM((2 * n, C), BF16),
        pltpu.VMEM((2 * n, C), BF16),
        pltpu.VMEM((2 * n, 3 * C), BF16),
    ]


class Reduction:
    count = 13

    @staticmethod
    def buffers(pairs, xp):
        n, nx = pairs * 16, xp * 16
        ny = n - nx
        shapes = [
            (pairs, 2, 16, 16),
            (pairs, 16, 16),
            (4, 4, nx), (4, 4, ny),
            (3, 4, nx), (3, 4, ny),
            (3, nx), (3, ny),
            (n,),
            (8, n),
            (n,),
        ]
        return [pltpu.VMEM(s + (C,), BF16) for s in shapes] + [dma(pairs + 7), dma(pairs + 7)]

    def __init__(self, pairs, xp, bufs, tm, rows):
        self.pairs, self.xp = pairs, xp
        self.n, self.nx = pairs * 16, xp * 16
        self.cut = self.nx
        self.packed, self.r1, self.ax1, self.ay1 = bufs[0:4]
        self.rx2, self.ry2, self.rx3, self.ry3, self.a3, self.r4, self.out = bufs[4:11]
        self.ss, self.rs = bufs[11:13]
        self.core, self.y, self.z_hi = lax.rem(tm, 2), lax.rem(tm // 2, 4), tm // 8
        self.x, self.z_lo = lax.rem(rows, 4), rows // 4
        self.tm, self.rows = tm, rows

    def copy(self, src, dst, s, r, device):
        return remote(
            src, dst, self.ss.at[self.pairs + s], self.rs.at[self.pairs + r], device
        )

    def tm_at(self, z_hi, y):
        return {"tm": z_hi * 8 + y * 2 + self.core}

    def row_at(self, z_lo, x):
        return {"rows": z_lo * 4 + x}

    def first(self, j):
        other = {"tm": self.tm + 1 - 2 * self.core}
        return remote(
            self.packed.at[j, 1 - self.core], self.r1.at[j], self.ss.at[j], self.rs.at[j], other
        )

    def send(self, j, upper, lower):
        for t in range(T):
            both = jnp.concatenate([upper[t * 8 : t * 8 + 8], lower[t * 8 : t * 8 + 8]], axis=0)
            self.packed[j, t % 2, t // 2] = both.astype(BF16)
        self.first(j).start()

    def second_x(self, s):
        x = lax.rem(self.x + s, 4)
        return self.copy(self.ax1.at[x], self.rx2.at[s - 1], 0, 0, self.row_at(self.z_lo, x))

    def second_y(self, s):
        y = lax.rem(self.y + s, 4)
        return self.copy(self.ay1.at[y], self.ry2.at[s - 1], 1, 1, self.tm_at(self.z_hi, y))

    def third_x(self, s):
        y = lax.rem(self.y + s, 4)
        return self.copy(
            self.ax1.at[self.x, y], self.rx3.at[s - 1], 2, 2, self.tm_at(self.z_hi, y)
        )

    def third_y(self, s):
        x = lax.rem(self.x + s, 4)
        return self.copy(
            self.ay1.at[self.y, x], self.ry3.at[s - 1], 3, 3, self.row_at(self.z_lo, x)
        )

    def piece(self, k):
        return pl.ds(0, self.cut) if k == 0 else pl.ds(self.cut, self.n - self.cut)

    def fourth(self, k):
        z = self.z_hi * 2 + self.z_lo
        at = self.piece(k)
        device = {"tm": self.x * 8 + self.y * 2 + self.core, "rows": k * 4 + self.x}
        return self.copy(self.a3.at[at], self.r4.at[z, at], 4 + k, 4, device)

    def fifth(self, k, s):
        at = self.piece(k)
        peer = lax.rem(self.rows + s, R)
        return self.copy(self.out.at[at], self.out.at[at], 6, 5 + k, {"rows": peer})

    def wait(self, src, dst, s, r, send=True, recv=True):
        copy = self.copy(src, dst, s, r, {"rows": lax.rem(self.rows + 1, R)})
        if send:
            copy.wait_send()
        if recv:
            copy.wait_recv()

    def holds(self, k):
        return jnp.logical_and(self.z_hi == self.x, self.z_lo == k)

    def away(self, k):
        return jnp.logical_not(self.holds(k))

    def after_core(self):
        for j in range(self.pairs):
            self.first(j).wait()
            in_x = j < self.xp
            at = pl.ds((j if in_x else j - self.xp) * 16, 16)

            def add(k, _):
                z, y = k // 4, lax.rem(k, 4)
                total = self.packed[j, self.core, k].astype(F32) + self.r1[j, k].astype(F32)
                if in_x:
                    self.ax1[z, y, at, :] = total.astype(BF16)
                else:
                    self.ay1[y, z, at, :] = total.astype(BF16)
                return 0

            lax.fori_loop(0, 16, add, 0, unroll=4)
            if j == self.xp - 1:
                for s in (1, 2, 3):
                    self.second_x(s).start()
        for s in (1, 2, 3):
            self.second_y(s).start()

    def after_second(self):
        for a, r, me, i, go in (
            (self.ax1, self.rx2, self.x, 0, self.third_x),
            (self.ay1, self.ry2, self.y, 1, self.third_y),
        ):
            self.wait(r, r, i, i)
            for j in range(4):
                total = a[me, j].astype(F32)
                for s in range(3):
                    total += r[s, j].astype(F32)
                a[me, j] = total.astype(BF16)
            for s in (1, 2, 3):
                go(s).start()

    def after_third(self):
        for a, r, i, j, at, sem in (
            (self.ax1, self.rx3, self.x, self.y, pl.ds(0, self.nx), 2),
            (self.ay1, self.ry3, self.y, self.x, pl.ds(self.nx, self.n - self.nx), 3),
        ):
            self.wait(r, r, sem, sem)
            total = a[i, j].astype(F32)
            for s in range(3):
                total += r[s].astype(F32)
            self.a3[at, :] = total.astype(BF16)
        for k in range(2):

            @pl.when(self.away(k))
            def _():
                self.fourth(k).start()

    def after_fourth(self):
        for k in range(2):

            @pl.when(self.away(k))
            def _():
                self.fourth(k).wait_send()

            @pl.when(self.holds(k))
            def _():
                at = self.piece(k)
                mine = self.z_hi * 2 + k
                seven = self.r4.at[pl.ds(0, 7), at]
                self.wait(seven, seven, 4, 4, send=False)
                self.r4[mine, at, :] = self.a3[at, :]
                total = self.r4[0, at, :].astype(F32)
                for z in range(1, 8):
                    total += self.r4[z, at, :].astype(F32)
                self.out[at, :] = total.astype(BF16)
                for s in range(1, R):
                    self.fifth(k, s).start()

    def finish(self):
        for k in range(2):

            @pl.when(self.holds(k))
            def _():
                seven = self.r4.at[pl.ds(0, 7), self.piece(k)]
                self.wait(seven, seven, 6, 5 + k, recv=False)

            @pl.when(self.away(k))
            def _():
                self.fifth(k, 1).wait_recv()

        return self.out[...].astype(F32) * (float(T * NR * R * W) ** -0.5)


def zero_at(ref, where, condition):
    @pl.when(condition)
    def _():
        ref[where] = jnp.zeros(ref[where].shape, ref.dtype)


def block_kernel(
    x_hbm, g_hbm, w_hbm, aw_hbm,
    dx, dconv, dattn,
    xe, ae, hid, w_ref, kt, aw, joined, gpad, gt, mpad, mt, pt, gm,
    xc, ac, ge, uc, pre, pc, g1,
    gs, gr, ms, mr, ps, pr, hs, hr, ks, kr, ls,
    *bufs,
):
    tm, rows = lax.axis_index("tm"), lax.axis_index("rows")
    up = {"rows": lax.rem(rows + R - 1, R)}
    down = {"rows": lax.rem(rows + 1, R)}
    top, bottom = rows == 0, rows == R - 1
    work, bufs = bufs[:10], bufs[10:]
    attn = Reduction(2, 1, bufs[:13], tm, rows)
    early = Reduction(4, 2, bufs[13:26], tm, rows)
    late = Reduction(5, 3, bufs[26:], tm, rows)
    g_bufs, m_bufs, p_bufs = (gpad, gt, gs, gr), (mpad, mt, ms, mr), (pt, gm, ps, pr)

    loads = [
        pltpu.make_async_copy(x_hbm, xe.at[pl.ds(2, NR)], ls.at[0]),
        pltpu.make_async_copy(g_hbm.at[pl.ds(0, 10)], gpad.at[0, pl.ds(0, 10)], ls.at[1]),
        pltpu.make_async_copy(g_hbm.at[pl.ds(40, 20)], gpad.at[0, pl.ds(10, 20)], ls.at[2]),
        pltpu.make_async_copy(g_hbm.at[pl.ds(10, 30)], gpad.at[1, pl.ds(0, 30)], ls.at[3]),
        pltpu.make_async_copy(w_hbm, w_ref, ls.at[4]),
        pltpu.make_async_copy(aw_hbm, aw, ls.at[5]),
    ]
    for load in loads:
        load.start()
    for half in range(2):
        gpad[half, 30:32] = jnp.zeros((2, PIX, C), BF16)
        mpad[half, 30:32] = jnp.zeros((2, PIX, C), BF16)
    barrier(tm, rows)
    loads[0].wait()
    to_up = remote(xe.at[pl.ds(2, 2)], xe.at[pl.ds(NR + 2, 2)], hs.at[0], hr.at[0], up)
    to_down = remote(xe.at[pl.ds(NR, 2)], xe.at[pl.ds(0, 2)], hs.at[1], hr.at[1], down)
    to_up.start()
    to_down.start()
    for load in loads[1:4]:
        load.wait()
    spread_start(g_bufs, 0, tm)
    fill(xe, xc, 2, NR, True)

    def keep(first, hidden):
        hid[first : first + hidden.shape[0]] = hidden
        ae[first : first + hidden.shape[0]] = (hidden * jax.nn.sigmoid(hidden)).astype(BF16)

    loads[4].wait()
    keep(2, conv(xc, ((2, 4),), w_ref[0], True))
    spread_start(g_bufs, 1, tm)
    to_up.wait()
    to_down.wait()
    zero_at(xe, slice(0, 2), top)
    zero_at(xe, slice(NR + 2, NR + 4), bottom)
    fill(xe, xc, 0, 2, True)
    fill(xe, xc, NR + 2, 2, True)
    ends = conv(xc, ((0, 2), (6, 2)), w_ref[0], True)
    keep(0, ends[0:2])
    keep(6, ends[2:4])
    zero_at(ae, slice(0, 1), top)
    zero_at(ae, slice(NR + 1, NR + 2), bottom)
    fill(ae, ac, 0, NR + 2, True)
    branch = conv(ac, ((0, 1), (4, 2)), w_ref[1], True)
    mixed = jnp.concatenate([xe[2:3], xe[6:8]], axis=0).astype(F32) + branch
    mpad[0, 0:30] = mixed.astype(BF16).reshape(30, PIX, C)
    spread_start(m_bufs, 0, tm)
    mixed = xe[3:6].astype(F32) + conv(ac, ((1, 3),), w_ref[1], True)
    mpad[1, 0:30] = mixed.astype(BF16).reshape(30, PIX, C)
    loads[5].wait()
    joined[...] = jnp.concatenate([aw[0], aw[1], aw[2]], axis=1)

    def turn(i, _):
        for k in range(2):
            at = pl.ds(pl.multiple_of(i * C, C), C)
            kt[k, at, :] = w_ref[k, at, :].astype(F32).T.astype(BF16)
        return 0

    lax.fori_loop(0, 9, turn, 0)

    def slopes(i, _):
        h = hid[i]
        s = jax.nn.sigmoid(h)
        hid[i] = s * (1.0 + h * (1.0 - s))
        return 0

    lax.fori_loop(0, NR + 2, slopes, 0)
    spread_wait(g_bufs, 0, tm)
    spread_wait(g_bufs, 1, tm)
    spread_start(m_bufs, 1, tm)
    for half in range(2):
        spread_wait(m_bufs, half, tm)
        attend(half, mt, gt, pt, aw, joined, work, UNROLL)
        spread_start(p_bufs, half, tm)

    gup, normed, att, gj = work[6:10]
    proj = tn(normed[...], gj[...])
    attn.send(0, proj[:, 0:C], proj[:, C : 2 * C])
    attn.send(1, proj[:, 2 * C : 3 * C], tn(att[...], gup[...]))

    spread_wait(p_bufs, 0, tm)
    ge[2:3] = gm[0, 0:10].reshape(1, W, C)
    ge[6:8] = gm[0, 10:30].reshape(2, W, C)
    near_up = remote(ge.at[2], ge.at[NR + 2], ks.at[0], kr.at[0], up)
    near_down = remote(ge.at[NR + 1], ge.at[1], ks.at[1], kr.at[1], down)
    near_up.start()
    near_down.start()
    fill(ge, uc, 2, 1, False)
    fill(ge, uc, 6, 2, False)

    def stacked(ref, runs):
        return jnp.concatenate([ref[s : s + n].reshape(n * W, ref.shape[2]) for s, n in runs], axis=0)

    for a in range(3):
        g1[a] = tn(stacked(ae, ((a, 1), (a + 4, 2))), stacked(uc, ((2, 1), (6, 2))))
    attn.after_core()

    def one(k):
        return g1[k // 3, :, (k % 3) * C : (k % 3 + 1) * C]

    spread_wait(p_bufs, 1, tm)
    ge[3:6] = gm[1, 0:30].reshape(3, W, C)
    far_up = remote(ge.at[3], ge.at[NR + 3], ks.at[2], kr.at[2], up)
    far_down = remote(ge.at[NR], ge.at[0], ks.at[3], kr.at[3], down)
    far_up.start()
    far_down.start()
    fill(ge, uc, 3, 3, False)
    for a in range(3):
        g1[a] += tn(stacked(ae, ((a + 1, 3),)), stacked(uc, ((3, 3),)))
        for j in ((0,), (1, 2), (3,))[a]:
            early.send(j, one(2 * j), one(2 * j + 1))

    def back(first, act_grad):
        at = slice(first, first + act_grad.shape[0])
        pre[at] = (act_grad.astype(BF16).astype(F32) * hid[at]).astype(BF16)

    near_up.wait()
    near_down.wait()
    zero_at(ge, slice(1, 2), top)
    zero_at(ge, slice(NR + 2, NR + 3), bottom)
    fill(ge, uc, 1, 1, False)
    fill(ge, uc, NR + 2, 1, False)
    back(1, conv(uc, ((1, 6),), kt[1], False))
    attn.after_second()
    early.after_core()
    fill(pre, pc, 1, NR, False)
    g0 = []

    def zero(k):
        return g0[k // 3][:, (k % 3) * C : (k % 3 + 1) * C]

    for a in range(3):
        g0.append(
            tn(xe[a + 1 : a + 1 + NR].reshape(NR * W, C), pc[1 : NR + 1].reshape(NR * W, 3 * C))
        )
        for j in ((0,), (1, 2), (3, 4))[a]:
            late.send(j, zero(2 * j), zero(2 * j + 1) if j < 4 else one(8))
    far_up.wait()
    far_down.wait()
    zero_at(ge, slice(0, 1), top)
    zero_at(ge, slice(NR + 3, NR + 4), bottom)
    fill(ge, uc, 0, 1, False)
    fill(ge, uc, NR + 3, 1, False)
    late.after_core()
    attn.after_third()
    ends = conv(uc, ((0, 1), (7, 1)), kt[1], False)
    back(0, ends[0:1])
    back(7, ends[1:2])
    zero_at(pre, slice(0, 1), top)
    zero_at(pre, slice(NR + 1, NR + 2), bottom)
    fill(pre, pc, 0, 1, False)
    fill(pre, pc, NR + 1, 1, False)
    early.after_second()
    attn.after_fourth()
    dx[...] = (ge[2:8].astype(F32) + conv(pc, ((0, 6),), kt[0], False)).astype(BF16)
    late.after_second()
    early.after_third()
    late.after_third()
    early.after_fourth()
    late.after_fourth()
    dattn[...] = attn.finish().reshape(4, 8, C)
    dconv[1, 0:8] = early.finish().reshape(8, 8, C)
    sums = late.finish()
    dconv[0] = sums[0:72].reshape(9, 8, C)
    dconv[1, 8:9] = sums[72:80].reshape(1, 8, C)


def pass_kernel(a, b, c, x, y, z):
    x[...] = a[...]
    y[...] = b[...]
    z[...] = c[...]


def anywhere(count):
    return [pl.BlockSpec(memory_space=pl.ANY)] * count


def vmem(count):
    return [pl.BlockSpec(memory_space=pltpu.VMEM)] * count


def dma(*shape):
    return pltpu.SemaphoreType.DMA(shape)


def params(collective_id=None):
    if collective_id is None:
        return pltpu.CompilerParams(vmem_limit_bytes=VMEM_LIMIT)
    return pltpu.CompilerParams(
        vmem_limit_bytes=VMEM_LIMIT, collective_id=collective_id, has_side_effects=True
    )


def per_device(frames_in, grad_out, conv_weight, attn_weight):
    x = frames_in.reshape(NR, W, C)
    g = grad_out.reshape(NR * W // PIX, PIX, C)
    w = conv_weight.reshape(2, 9 * C, C)
    spread = pltpu.VMEM((2, T, PIX, C), BF16)
    shapes = [
        jax.ShapeDtypeStruct((NR, W, C), BF16),
        jax.ShapeDtypeStruct((2, 9, 8, C), F32),
        jax.ShapeDtypeStruct((4, 8, C), F32),
    ]
    outs = pl.pallas_call(
        block_kernel,
        out_shape=shapes,
        in_specs=anywhere(4),
        out_specs=vmem(3),
        scratch_shapes=[
            pltpu.VMEM((NR + 4, W, C), BF16),
            pltpu.VMEM((NR + 2, W, C), BF16),
            pltpu.VMEM((NR + 2, W, C), F32),
            pltpu.VMEM((2, 9 * C, C), BF16),
            pltpu.VMEM((2, 9 * C, C), BF16),
            pltpu.VMEM((4, C, C), BF16),
            pltpu.VMEM((C, 3 * C), BF16),
            *[spread] * 6,
            pltpu.VMEM((NR + 4, W, 3 * C), BF16),
            pltpu.VMEM((NR + 2, W, 3 * C), BF16),
            pltpu.VMEM((NR + 4, W, C), BF16),
            pltpu.VMEM((NR + 4, W, 3 * C), BF16),
            pltpu.VMEM((NR + 2, W, C), BF16),
            pltpu.VMEM((NR + 2, W, 3 * C), BF16),
            pltpu.VMEM((3, C, 3 * C), F32),
            *[dma(2)] * 6,
            dma(2), dma(2), dma(4), dma(4), dma(6),
            *attend_buffers(),
            *Reduction.buffers(2, 1),
            *Reduction.buffers(4, 2),
            *Reduction.buffers(5, 3),
        ],
        compiler_params=params(1),
        name="block",
    )(x, g, w, attn_weight)
    dx, dconv, dattn = pl.pallas_call(
        pass_kernel,
        out_shape=shapes,
        in_specs=vmem(3),
        out_specs=vmem(3),
        compiler_params=params(),
        name="hand_on",
    )(*outs)
    return dx.reshape(1, NR, W, C), dconv, dattn


def solution(mesh):
    return jax.shard_map(
        per_device,
        mesh=mesh,
        in_specs=(P("tm", "rows", None, None), P("tm", "rows", None, None), P(), P()),
        out_specs=(P("tm", "rows", None, None), P(None, None, "tm", None), P(None, "tm", None)),
        check_vma=False,
    )
```

```python
import functools

import jax
import jax.numpy as jnp
from jax import lax
from jax.experimental import pallas as pl
from jax.experimental.pallas import tpu as pltpu
from jax.sharding import PartitionSpec as P

HEADS = 4
EPSILON = 1e-06
T, R = 32, 8
NR, W, C = 6, 160, 256
PIX = 16
UNROLL = 4
F32, BF16 = jnp.float32, jnp.bfloat16
MESH = pl.DeviceIdType.MESH
VMEM_LIMIT = 60 * 1024 * 1024


def signal(sem, device):
    pl.semaphore_signal(sem, inc=1, device_id=device, device_id_type=MESH)


def barrier(tm, rows):
    sem = pltpu.get_barrier_semaphore()

    def tell_tm(s, _):
        signal(sem, {"tm": lax.rem(tm + s, T)})
        return 0

    lax.fori_loop(1, T, tell_tm, 0)
    for s in range(1, R):
        signal(sem, {"rows": lax.rem(rows + s, R)})
    for s in (8, 16, 24):
        signal(sem, {"tm": lax.rem(tm + s, T), "rows": lax.rem(rows + 4, R)})
    pl.semaphore_wait(sem, T - 1 + R - 1 + 3)


def remote(src, dst, ss, rs, device):
    return pltpu.make_async_remote_copy(
        src_ref=src,
        dst_ref=dst,
        send_sem=ss,
        recv_sem=rs,
        device_id=device,
        device_id_type=MESH,
    )


def spread_start(bufs, half, tm):
    src, dst, ss, rs = bufs

    def go(s, _):
        peer = lax.rem(tm + s, T)
        remote(
            src.at[half, peer], dst.at[half, tm], ss.at[half], rs.at[half], {"tm": peer}
        ).start()
        return 0

    lax.fori_loop(1, T, go, 0)
    dst[half, tm] = src[half, tm]


def spread_wait(bufs, half, tm):
    src, dst, ss, rs = bufs
    every = pl.ds(0, T - 1)
    copy = remote(
        src.at[half, every], dst.at[half, every], ss.at[half], rs.at[half],
        {"tm": lax.rem(tm + 1, T)},
    )
    copy.wait_send()
    copy.wait_recv()


def shifts(row):
    col = lax.broadcasted_iota(jnp.int32, (W, C), 0)
    before = jnp.where(col == 0, 0.0, pltpu.roll(row, 1, 0))
    after = jnp.where(col == W - 1, 0.0, pltpu.roll(row, W - 1, 0))
    return before, row, after


def fill(src, dst, first, count, forward):
    def go(i, _):
        before, here, after = shifts(src[i].astype(F32))
        parts = (before, here, after) if forward else (after, here, before)
        for b in range(3):
            dst[i, :, b * C : (b + 1) * C] = parts[b].astype(BF16)
        return 0

    lax.fori_loop(first, first + count, go, 0)


def taps(wide, start, count, forward):
    pieces = []
    for a in range(3):
        off = a if forward else 2 - a
        pieces.append(wide[start + off : start + off + count].reshape(count * W, 3 * C))
    return jnp.concatenate(pieces, axis=1)


def conv(wide, runs, weight, forward):
    lhs = [taps(wide, start, count, forward) for start, count in runs]
    lhs = lhs[0] if len(lhs) == 1 else jnp.concatenate(lhs, axis=0)
    out = jnp.dot(lhs, weight, preferred_element_type=F32)
    return out.reshape(out.shape[0] // W, W, C)


def nt(a, b):
    return lax.dot_general(a, b, (((1,), (1,)), ((), ())), preferred_element_type=F32)


def tn(a, b):
    return lax.dot_general(a, b, (((0,), (0,)), ((), ())), preferred_element_type=F32)


def attend(half, mt, gt, pt, aw, joined, work, unroll):
    stage, stage_g, mix, scale, qkv, ga, gup, normed, att, gj = work
    n = T * PIX
    base = half * n

    def widen(f, _):
        at = pl.ds(pl.multiple_of(f * PIX, PIX), PIX)
        for h in range(2):
            cols = pl.ds(h * 128, 128)
            stage[h, at, :] = mt[half, f, :, cols].astype(F32)
            stage_g[h, at, :] = gt[half, f, :, cols].astype(F32)
        return 0

    lax.fori_loop(0, T, widen, 0, unroll=4)

    def by_pixel(p, _):
        at = pl.ds(pl.multiple_of(p * T, T), T)
        to = pl.ds(pl.multiple_of(base + p * T, T), T)
        m = jnp.concatenate([stage[h, pl.ds(p, T, stride=PIX), :] for h in range(2)], axis=1)
        g = jnp.concatenate([stage_g[h, pl.ds(p, T, stride=PIX), :] for h in range(2)], axis=1)
        ns = lax.rsqrt(jnp.mean(m * m, axis=-1, keepdims=True) + EPSILON)
        mix[at, :] = m
        scale[at, :] = jnp.broadcast_to(ns, (T, 128))
        normed[to, :] = (m * ns).astype(BF16)
        gup[to, :] = g.astype(BF16)
        return 0

    lax.fori_loop(0, PIX, by_pixel, 0, unroll=4)
    every = pl.ds(base, n)
    qkv[...] = jnp.dot(normed[every, :], joined[...], preferred_element_type=F32).astype(BF16)
    ga[...] = nt(gup[every, :], aw[3]).astype(BF16)

    factor = 64.0**-0.5
    g = 128
    lane = lax.broadcasted_iota(jnp.int32, (1, C), 1) // 64
    head = [(lane == h).astype(F32).astype(BF16) for h in range(HEADS)]
    blocks = (
        lax.rem(lax.broadcasted_iota(jnp.int32, (HEADS * g, g), 0), g) // T
        == lax.broadcasted_iota(jnp.int32, (HEADS * g, g), 1) // T
    )

    def stack(x):
        return jnp.concatenate([x * head[h] for h in range(HEADS)], axis=0)

    def side(x):
        return jnp.concatenate([x[h * g : (h + 1) * g] for h in range(HEADS)], axis=1)

    def group(i, _):
        at = pl.ds(pl.multiple_of(i * g, g), g)
        to = pl.ds(pl.multiple_of(base + i * g, g), g)
        q, k, v = qkv[at, 0:C], qkv[at, C : 2 * C], qkv[at, 2 * C : 3 * C]
        qs, ks, vs, gas = stack(q), stack(k), stack(v), stack(ga[at, :])
        expo = jnp.where(blocks, jnp.exp(nt(qs, k) * factor), 0.0)
        probs = expo / jnp.sum(expo, axis=-1, keepdims=True)
        low = probs.astype(BF16)
        att[to, :] = jnp.dot(side(low), vs, preferred_element_type=F32).astype(BF16)
        gp = nt(gas, v)
        gs = probs * (gp - jnp.sum(probs * gp, axis=-1, keepdims=True))
        sl = (gs * factor).astype(BF16)
        gj[to, 0:C] = jnp.dot(side(sl), ks, preferred_element_type=F32).astype(BF16)
        gj[to, C : 2 * C] = tn(sl, qs).astype(BF16)
        gj[to, 2 * C : 3 * C] = tn(low, gas).astype(BF16)
        return 0

    lax.fori_loop(0, n // g, group, 0, unroll=unroll)
    step = 256
    for i in range(n // step):
        at = slice(i * step, (i + 1) * step)
        to = slice(base + i * step, base + (i + 1) * step)
        gn = nt(gj[to, :], joined[...])
        m = mix[at, :]
        ns = jnp.concatenate([scale[at, :]] * 2, axis=1)
        inner = jnp.mean(gn * m, axis=-1, keepdims=True)
        total = gup[to, :].astype(F32) + (ns * gn - m * ns * ns * ns * inner)
        for h in range(2):
            stage[h, at, :] = total[:, h * 128 : (h + 1) * 128]

    def by_frame(f, _):
        for h in range(2):
            pt[half, f, :, pl.ds(h * 128, 128)] = stage[h, pl.ds(f, PIX, stride=T), :].astype(BF16)
        return 0

    lax.fori_loop(0, T, by_frame, 0, unroll=4)


def attend_buffers():
    n = T * PIX
    return [
        pltpu.VMEM((2, n, 128), F32),
        pltpu.VMEM((2, n, 128), F32),
        pltpu.VMEM((n, C), F32),
        pltpu.VMEM((n, 128), F32),
        pltpu.VMEM((n, 3 * C), BF16),
        pltpu.VMEM((n, C), BF16),
        pltpu.VMEM((2 * n, C), BF16),
        pltpu.VMEM((2 * n, C), BF16),
        pltpu.VMEM((2 * n, C), BF16),
        pltpu.VMEM((2 * n, 3 * C), BF16),
    ]


class Reduction:
    @staticmethod
    def buffers(pairs, xp, joint):
        n, nx = pairs * 16, xp * 16
        ny = n - nx
        shapes = [
            *(() if joint else ((pairs, 2, 16, 16), (pairs, 16, 16))),
            (4, 4, nx), (4, 4, ny),
            (3, 4, nx), (3, 4, ny),
            (3, nx), (3, ny),
            (n,),
            (8, n),
            (n,),
        ]
        return [pltpu.VMEM(s + (C,), BF16) for s in shapes] + [dma(7 if joint else pairs + 7)] * 2

    def __init__(self, pairs, xp, joint, bufs, tm, rows):
        self.pairs, self.xp, self.joint = pairs, xp, joint
        self.skip = 0 if joint else pairs
        if not joint:
            self.packed, self.r1 = bufs[0:2]
            bufs = bufs[2:]
        self.n, self.nx = pairs * 16, xp * 16
        self.cut = self.nx
        self.ax1, self.ay1, self.rx2, self.ry2, self.rx3, self.ry3 = bufs[0:6]
        self.a3, self.r4, self.out, self.ss, self.rs = bufs[6:11]
        self.core, self.y, self.z_hi = lax.rem(tm, 2), lax.rem(tm // 2, 4), tm // 8
        self.x, self.z_lo = lax.rem(rows, 4), rows // 4
        self.tm, self.rows = tm, rows

    def copy(self, src, dst, s, r, device):
        return remote(
            src, dst, self.ss.at[self.skip + s], self.rs.at[self.skip + r], device
        )

    def tm_at(self, z_hi, y):
        return {"tm": z_hi * 8 + y * 2 + self.core}

    def row_at(self, z_lo, x):
        return {"rows": z_lo * 4 + x}

    def first(self, j):
        other = {"tm": self.tm + 1 - 2 * self.core}
        return remote(
            self.packed.at[j, 1 - self.core], self.r1.at[j], self.ss.at[j], self.rs.at[j], other
        )

    def place(self, j):
        in_x = j < self.xp
        return self.ax1 if in_x else self.ay1, pl.ds((j if in_x else j - self.xp) * 16, 16)

    def send_on(self, j):
        if j == self.xp - 1 or j == self.pairs - 1:
            for s in (1, 2, 3):
                (self.second_x if j < self.xp else self.second_y)(s).start()

    def send(self, j, upper, lower):
        for t in range(T // 2 if self.joint else T):
            both = jnp.concatenate([upper[t * 8 : t * 8 + 8], lower[t * 8 : t * 8 + 8]], axis=0)
            core, t = (0, t) if self.joint else (t % 2, t // 2)
            z, y = t // 4, t % 4
            k = z * 4 + y if j < self.xp else y * 4 + z
            if self.joint:
                to, at = self.place(j)
                to[k // 4, k % 4, at, :] = both.astype(BF16)
            else:
                self.packed[j, core, k] = both.astype(BF16)
        if self.joint:
            self.send_on(j)
        else:
            self.first(j).start()

    def second_x(self, s):
        x = lax.rem(self.x + s, 4)
        return self.copy(self.ax1.at[x], self.rx2.at[s - 1], 0, 0, self.row_at(self.z_lo, x))

    def second_y(self, s):
        y = lax.rem(self.y + s, 4)
        return self.copy(self.ay1.at[y], self.ry2.at[s - 1], 1, 1, self.tm_at(self.z_hi, y))

    def third_x(self, s):
        y = lax.rem(self.y + s, 4)
        return self.copy(
            self.ax1.at[self.x, y], self.rx3.at[s - 1], 2, 2, self.tm_at(self.z_hi, y)
        )

    def third_y(self, s):
        x = lax.rem(self.x + s, 4)
        return self.copy(
            self.ay1.at[self.y, x], self.ry3.at[s - 1], 3, 3, self.row_at(self.z_lo, x)
        )

    def piece(self, k):
        return pl.ds(0, self.cut) if k == 0 else pl.ds(self.cut, self.n - self.cut)

    def fourth(self, k):
        z = self.z_hi * 2 + self.z_lo
        at = self.piece(k)
        device = {"tm": self.x * 8 + self.y * 2 + self.core, "rows": k * 4 + self.x}
        return self.copy(self.a3.at[at], self.r4.at[z, at], 4 + k, 4, device)

    def fifth(self, k, s):
        at = self.piece(k)
        peer = lax.rem(self.rows + s, R)
        return self.copy(self.out.at[at], self.out.at[at], 6, 5 + k, {"rows": peer})

    def wait(self, src, dst, s, r, send=True, recv=True):
        copy = self.copy(src, dst, s, r, {"rows": lax.rem(self.rows + 1, R)})
        if send:
            copy.wait_send()
        if recv:
            copy.wait_recv()

    def holds(self, k):
        return jnp.logical_and(self.z_hi == self.x, self.z_lo == k)

    def away(self, k):
        return jnp.logical_not(self.holds(k))

    def after_core(self):
        for j in range(self.pairs):
            self.first(j).wait()
            to, at = self.place(j)
            total = self.packed[j, self.core].astype(F32) + self.r1[j].astype(F32)
            to[:, :, at, :] = total.astype(BF16).reshape(4, 4, 16, C)
            self.send_on(j)

    def after_second(self):
        for a, r, me, i, go in (
            (self.ax1, self.rx2, self.x, 0, self.third_x),
            (self.ay1, self.ry2, self.y, 1, self.third_y),
        ):
            self.wait(r, r, i, i)
            total = a[me].astype(F32)
            for s in range(3):
                total += r[s].astype(F32)
            a[me] = total.astype(BF16)
            for s in (1, 2, 3):
                go(s).start()

    def after_third(self):
        for a, r, i, j, at, sem in (
            (self.ax1, self.rx3, self.x, self.y, pl.ds(0, self.nx), 2),
            (self.ay1, self.ry3, self.y, self.x, pl.ds(self.nx, self.n - self.nx), 3),
        ):
            self.wait(r, r, sem, sem)
            total = a[i, j].astype(F32)
            for s in range(3):
                total += r[s].astype(F32)
            self.a3[at, :] = total.astype(BF16)
        for k in range(2):

            @pl.when(self.away(k))
            def _():
                self.fourth(k).start()

    def after_fourth(self):
        for k in range(2):

            @pl.when(self.away(k))
            def _():
                self.fourth(k).wait_send()

            @pl.when(self.holds(k))
            def _():
                at = self.piece(k)
                mine = self.z_hi * 2 + k
                seven = self.r4.at[pl.ds(0, 7), at]
                self.wait(seven, seven, 4, 4, send=False)
                self.r4[mine, at, :] = self.a3[at, :]
                total = self.r4[0, at, :].astype(F32)
                for z in range(1, 8):
                    total += self.r4[z, at, :].astype(F32)
                self.out[at, :] = total.astype(BF16)
                for s in range(1, R):
                    self.fifth(k, s).start()

    def finish(self):
        for k in range(2):

            @pl.when(self.holds(k))
            def _():
                seven = self.r4.at[pl.ds(0, 7), self.piece(k)]
                self.wait(seven, seven, 6, 5 + k, recv=False)

            @pl.when(self.away(k))
            def _():
                self.fifth(k, 1).wait_recv()

        return self.out[...].astype(F32) * (float(T * NR * R * W) ** -0.5)


def zero_at(ref, where, condition):
    @pl.when(condition)
    def _():
        ref[where] = jnp.zeros(ref[where].shape, ref.dtype)


def block_kernel(
    x_hbm, g_hbm, w_hbm, aw_hbm,
    dx, dconv, dattn,
    xe, ae, hid, w_ref, kt, aw, joined, gpad, gt, mpad, mt, pt, gm,
    xc, ac, ge, uc, pre, pc, g1, xt, at0, at1, xs, as0, as1, u0, s0, u1, s1,
    gs, gr, ms, mr, ps, pr, hs, hr, ks, kr, ls, ts, tr,
    *bufs,
):
    tm, rows = lax.axis_index("tm"), lax.axis_index("rows")
    up = {"rows": lax.rem(rows + R - 1, R)}
    down = {"rows": lax.rem(rows + 1, R)}
    top, bottom = rows == 0, rows == R - 1
    work, bufs = bufs[:10], bufs[10:]
    attn = Reduction(2, 1, False, bufs[:13], tm, rows)
    early = Reduction(4, 2, True, bufs[13:24], tm, rows)
    late = Reduction(5, 3, True, bufs[24:], tm, rows)
    core = lax.rem(tm, 2)
    twin = {"tm": tm + 1 - 2 * core}
    g_bufs, m_bufs, p_bufs = (gpad, gt, gs, gr), (mpad, mt, ms, mr), (pt, gm, ps, pr)

    loads = [
        pltpu.make_async_copy(x_hbm, xe.at[pl.ds(2, NR)], ls.at[0]),
        pltpu.make_async_copy(g_hbm.at[pl.ds(0, 10)], gpad.at[0, pl.ds(0, 10)], ls.at[1]),
        pltpu.make_async_copy(g_hbm.at[pl.ds(40, 20)], gpad.at[0, pl.ds(10, 20)], ls.at[2]),
        pltpu.make_async_copy(g_hbm.at[pl.ds(10, 30)], gpad.at[1, pl.ds(0, 30)], ls.at[3]),
        pltpu.make_async_copy(w_hbm, w_ref, ls.at[4]),
        pltpu.make_async_copy(aw_hbm, aw, ls.at[5]),
    ]
    for load in loads:
        load.start()
    for half in range(2):
        gpad[half, 30:32] = jnp.zeros((2, PIX, C), BF16)
        mpad[half, 30:32] = jnp.zeros((2, PIX, C), BF16)
    barrier(tm, rows)
    loads[0].wait()
    to_up = remote(xe.at[pl.ds(2, 2)], xe.at[pl.ds(NR + 2, 2)], hs.at[0], hr.at[0], up)
    to_down = remote(xe.at[pl.ds(NR, 2)], xe.at[pl.ds(0, 2)], hs.at[1], hr.at[1], down)
    to_up.start()
    to_down.start()
    for load in loads[1:4]:
        load.wait()
    spread_start(g_bufs, 0, tm)
    fill(xe, xc, 2, NR, True)

    def keep(first, hidden):
        hid[first : first + hidden.shape[0]] = hidden
        ae[first : first + hidden.shape[0]] = (hidden * jax.nn.sigmoid(hidden)).astype(BF16)

    loads[4].wait()
    keep(2, conv(xc, ((2, 4),), w_ref[0], True))
    spread_start(g_bufs, 1, tm)
    to_up.wait()
    to_down.wait()
    zero_at(xe, slice(0, 2), top)
    zero_at(xe, slice(NR + 2, NR + 4), bottom)
    fill(xe, xc, 0, 2, True)
    fill(xe, xc, NR + 2, 2, True)
    ends = conv(xc, ((0, 2), (6, 2)), w_ref[0], True)
    keep(0, ends[0:2])
    keep(6, ends[2:4])
    zero_at(ae, slice(0, 1), top)
    zero_at(ae, slice(NR + 1, NR + 2), bottom)
    fill(ae, ac, 0, NR + 2, True)
    branch = conv(ac, ((0, 1), (4, 2)), w_ref[1], True)
    mixed = jnp.concatenate([xe[2:3], xe[6:8]], axis=0).astype(F32) + branch
    mpad[0, 0:30] = mixed.astype(BF16).reshape(30, PIX, C)
    spread_start(m_bufs, 0, tm)
    mixed = xe[3:6].astype(F32) + conv(ac, ((1, 3),), w_ref[1], True)
    mpad[1, 0:30] = mixed.astype(BF16).reshape(30, PIX, C)
    spread_wait(g_bufs, 0, tm)
    loads[5].wait()
    joined[...] = jnp.concatenate([aw[0], aw[1], aw[2]], axis=1)

    def turn(i, _):
        for k in range(2):
            at = pl.ds(pl.multiple_of(i * C, C), C)
            kt[k, at, :] = w_ref[k, at, :].astype(F32).T.astype(BF16)
        return 0

    lax.fori_loop(0, 9, turn, 0)

    def slopes(i, _):
        h = hid[i]
        s = jax.nn.sigmoid(h)
        hid[i] = s * (1.0 + h * (1.0 - s))
        return 0

    lax.fori_loop(0, NR + 2, slopes, 0)

    def flip(to, a, b, pieces, depth):
        rows_in = [p.reshape(-1, C).astype(F32) for p in pieces]
        short = depth - sum(p.shape[0] for p in rows_in)
        flat = jnp.concatenate(rows_in + [jnp.zeros((short, C), F32)], axis=0).T
        flat = flat.reshape(16, 2, 8, depth)
        for c in range(2):
            to[c, a, b * 128 : (b + 1) * 128, :] = flat[:, c].reshape(128, depth).astype(BF16)

    def flips(a, _):
        for b in range(3):
            at = pl.ds(b * C, C)
            flip(xt, a, b, [xc[pl.ds(a + 1, NR), :, at]], 1024)
            flip(at0, a, b, [ac[pl.ds(a, 1), :, at], ac[pl.ds(a + 4, 2), :, at]], 512)
            flip(at1, a, b, [ac[pl.ds(a + 1, 3), :, at]], 512)
        return 0

    lax.fori_loop(0, 3, flips, 0)
    swaps = [
        remote(src.at[1 - core], dst, ts.at[k], tr.at[k], twin)
        for k, (src, dst) in enumerate(((at0, as0), (at1, as1), (xt, xs)))
    ]
    for swap in swaps:
        swap.start()
    for buf in (u1, s1):
        buf[:, 480:512] = jnp.zeros((2, 32, C), BF16)
    for buf in (u0, s0):
        buf[960:1024] = jnp.zeros((64, C), BF16)
    full = pl.ds(0, 480)
    u_swaps = [
        remote(u1.at[0, full], s1.at[0, full], ts.at[3], tr.at[3], twin),
        remote(u1.at[1, full], s1.at[1, full], ts.at[4], tr.at[4], twin),
        remote(u0.at[pl.ds(0, 960)], s0.at[pl.ds(0, 960)], ts.at[5], tr.at[5], twin),
    ]
    spread_wait(g_bufs, 1, tm)
    spread_start(m_bufs, 1, tm)
    for half in range(2):
        spread_wait(m_bufs, half, tm)
        attend(half, mt, gt, pt, aw, joined, work, UNROLL)
        spread_start(p_bufs, half, tm)

    gup, normed, att, gj = work[6:10]
    proj = tn(normed[...], gj[...])
    attn.send(0, proj[:, 0:C], proj[:, C : 2 * C])
    attn.send(1, proj[:, 2 * C : 3 * C], tn(att[...], gup[...]))

    spread_wait(p_bufs, 0, tm)
    ge[2:3] = gm[0, 0:10].reshape(1, W, C)
    ge[6:8] = gm[0, 10:30].reshape(2, W, C)
    u1[0, 0:480] = gm[0, 0:30].reshape(480, C)
    u_swaps[0].start()
    near_up = remote(ge.at[2], ge.at[NR + 2], ks.at[0], kr.at[0], up)
    near_down = remote(ge.at[NR + 1], ge.at[1], ks.at[1], kr.at[1], down)
    near_up.start()
    near_down.start()
    fill(ge, uc, 2, 1, False)
    fill(ge, uc, 6, 2, False)

    def times(a, b):
        return jnp.dot(a, b, preferred_element_type=F32)

    for swap in swaps:
        swap.wait()
    u_swaps[0].wait()
    for a in range(3):
        g1[a] = times(at0[core, a], u1[0]) + times(as0[a], s1[0])
    attn.after_core()

    def one(k):
        return g1[k // 3, (k % 3) * 128 : (k % 3 + 1) * 128, :]

    spread_wait(p_bufs, 1, tm)
    ge[3:6] = gm[1, 0:30].reshape(3, W, C)
    u1[1, 0:480] = gm[1, 0:30].reshape(480, C)
    u_swaps[1].start()
    far_up = remote(ge.at[3], ge.at[NR + 3], ks.at[2], kr.at[2], up)
    far_down = remote(ge.at[NR], ge.at[0], ks.at[3], kr.at[3], down)
    far_up.start()
    far_down.start()
    fill(ge, uc, 3, 3, False)

    def back(first, act_grad):
        at = slice(first, first + act_grad.shape[0])
        pre[at] = (act_grad.astype(BF16).astype(F32) * hid[at]).astype(BF16)

    near_up.wait()
    near_down.wait()
    zero_at(ge, slice(1, 2), top)
    zero_at(ge, slice(NR + 2, NR + 3), bottom)
    fill(ge, uc, 1, 1, False)
    fill(ge, uc, NR + 2, 1, False)
    back(1, conv(uc, ((1, 6),), kt[1], False))
    u0[0:960] = pre[1 : NR + 1].reshape(960, C)
    u_swaps[2].start()
    u_swaps[1].wait()
    for a in range(3):
        g1[a] += times(at1[core, a], u1[1]) + times(as1[a], s1[1])
        for j in ((0,), (1, 2), (3,))[a]:
            early.send(j, one(2 * j), one(2 * j + 1))
    g0 = []

    def zero(k):
        return g0[k // 3][(k % 3) * 128 : (k % 3 + 1) * 128]

    u_swaps[2].wait()
    for a in range(3):
        g0.append(times(xt[core, a], u0[...]) + times(xs[a], s0[...]))
        for j in ((0,), (1, 2), (3, 4))[a]:
            late.send(j, zero(2 * j), zero(2 * j + 1) if j < 4 else one(8))
    attn.after_second()
    far_up.wait()
    far_down.wait()
    zero_at(ge, slice(0, 1), top)
    zero_at(ge, slice(NR + 3, NR + 4), bottom)
    fill(ge, uc, 0, 1, False)
    fill(ge, uc, NR + 3, 1, False)
    ends = conv(uc, ((0, 1), (7, 1)), kt[1], False)
    back(0, ends[0:1])
    back(7, ends[1:2])
    zero_at(pre, slice(0, 1), top)
    zero_at(pre, slice(NR + 1, NR + 2), bottom)
    fill(pre, pc, 0, NR + 2, False)
    early.after_second()
    dx[...] = (ge[2:8].astype(F32) + conv(pc, ((0, 6),), kt[0], False)).astype(BF16)
    attn.after_third()
    late.after_second()
    early.after_third()
    late.after_third()
    attn.after_fourth()
    early.after_fourth()
    late.after_fourth()
    dattn[...] = attn.finish().reshape(4, 8, C)
    dconv[1, 0:8] = early.finish().reshape(8, 8, C)
    sums = late.finish()
    dconv[0] = sums[0:72].reshape(9, 8, C)
    dconv[1, 8:9] = sums[72:80].reshape(1, 8, C)


def pass_kernel(a, b, c, x, y, z, va, vb, vc, sems):
    trips = [(a.at[i], va.at[i], x.at[i]) for i in range(NR)] + [(b, vb, y), (c, vc, z)]
    into = [pltpu.make_async_copy(s, v, sems.at[k]) for k, (s, v, _) in enumerate(trips)]
    out = [pltpu.make_async_copy(v, d, sems.at[8 + k]) for k, (_, v, d) in enumerate(trips)]
    for copy in into:
        copy.start()
    for k in range(8):
        into[k].wait()
        out[k].start()
    for copy in out:
        copy.wait()


def anywhere(count):
    return [pl.BlockSpec(memory_space=pl.ANY)] * count


def vmem(count):
    return [pl.BlockSpec(memory_space=pltpu.VMEM)] * count


def dma(*shape):
    return pltpu.SemaphoreType.DMA(shape)


def params(collective_id=None):
    if collective_id is None:
        return pltpu.CompilerParams(vmem_limit_bytes=VMEM_LIMIT)
    return pltpu.CompilerParams(
        vmem_limit_bytes=VMEM_LIMIT, collective_id=collective_id, has_side_effects=True
    )


def per_device(frames_in, grad_out, conv_weight, attn_weight):
    x = frames_in.reshape(NR, W, C)
    g = grad_out.reshape(NR * W // PIX, PIX, C)
    w = conv_weight.reshape(2, 9 * C, C)
    spread = pltpu.VMEM((2, T, PIX, C), BF16)
    shapes = [
        jax.ShapeDtypeStruct((NR, W, C), BF16),
        jax.ShapeDtypeStruct((2, 9, 8, C), F32),
        jax.ShapeDtypeStruct((4, 8, C), F32),
    ]
    outs = pl.pallas_call(
        block_kernel,
        out_shape=shapes,
        in_specs=anywhere(4),
        out_specs=vmem(3),
        scratch_shapes=[
            pltpu.VMEM((NR + 4, W, C), BF16),
            pltpu.VMEM((NR + 2, W, C), BF16),
            pltpu.VMEM((NR + 2, W, C), F32),
            pltpu.VMEM((2, 9 * C, C), BF16),
            pltpu.VMEM((2, 9 * C, C), BF16),
            pltpu.VMEM((4, C, C), BF16),
            pltpu.VMEM((C, 3 * C), BF16),
            *[spread] * 6,
            pltpu.VMEM((NR + 4, W, 3 * C), BF16),
            pltpu.VMEM((NR + 2, W, 3 * C), BF16),
            pltpu.VMEM((NR + 4, W, C), BF16),
            pltpu.VMEM((NR + 4, W, 3 * C), BF16),
            pltpu.VMEM((NR + 2, W, C), BF16),
            pltpu.VMEM((NR + 2, W, 3 * C), BF16),
            pltpu.VMEM((3, 384, C), F32),
            pltpu.VMEM((2, 3, 384, 1024), BF16),
            pltpu.VMEM((2, 3, 384, 512), BF16),
            pltpu.VMEM((2, 3, 384, 512), BF16),
            pltpu.VMEM((3, 384, 1024), BF16),
            pltpu.VMEM((3, 384, 512), BF16),
            pltpu.VMEM((3, 384, 512), BF16),
            pltpu.VMEM((1024, C), BF16),
            pltpu.VMEM((1024, C), BF16),
            pltpu.VMEM((2, 512, C), BF16),
            pltpu.VMEM((2, 512, C), BF16),
            *[dma(2)] * 6,
            dma(2), dma(2), dma(4), dma(4), dma(6), dma(6), dma(6),
            *attend_buffers(),
            *Reduction.buffers(2, 1, False),
            *Reduction.buffers(4, 2, True),
            *Reduction.buffers(5, 3, True),
        ],
        compiler_params=params(1),
        name="block",
    )(x, g, w, attn_weight)
    dx, dconv, dattn = pl.pallas_call(
        pass_kernel,
        out_shape=shapes,
        in_specs=anywhere(3),
        out_specs=anywhere(3),
        scratch_shapes=[*[pltpu.VMEM(s.shape, s.dtype) for s in shapes], dma(16)],
        compiler_params=params(),
        name="hand_on",
    )(*outs)
    return dx.reshape(1, NR, W, C), dconv, dattn


def solution(mesh):
    return jax.shard_map(
        per_device,
        mesh=mesh,
        in_specs=(P("tm", "rows", None, None), P("tm", "rows", None, None), P(), P()),
        out_specs=(P("tm", "rows", None, None), P(None, None, "tm", None), P(None, "tm", None)),
        check_vma=False,
    )
```

```python
import functools

import jax
import jax.numpy as jnp
from jax import lax
from jax.experimental import pallas as pl
from jax.experimental.pallas import tpu as pltpu
from jax.sharding import PartitionSpec as P

HEADS = 4
EPSILON = 1e-06
T, R = 32, 8
NR, W, C = 6, 160, 256
PIX = 16
UNROLL = 4
IDLE = ((0, 10), (20, 30))
RUNS = (((1, 0, 9), (11, 9, 21)), ((0, 0, 20), (21, 20, 9), (31, 29, 1)))
F32, BF16 = jnp.float32, jnp.bfloat16
MESH = pl.DeviceIdType.MESH
VMEM_LIMIT = 60 * 1024 * 1024


def signal(sem, device):
    pl.semaphore_signal(sem, inc=1, device_id=device, device_id_type=MESH)


def barrier(tm, rows):
    sem = pltpu.get_barrier_semaphore()

    def tell_tm(s, _):
        signal(sem, {"tm": lax.rem(tm + s, T)})
        return 0

    lax.fori_loop(1, T, tell_tm, 0)
    for s in range(1, R):
        signal(sem, {"rows": lax.rem(rows + s, R)})
    for s in (8, 16, 24):
        signal(sem, {"tm": lax.rem(tm + s, T), "rows": lax.rem(rows + 4, R)})
    pl.semaphore_wait(sem, T - 1 + R - 1 + 3)


def remote(src, dst, ss, rs, device):
    return pltpu.make_async_remote_copy(
        src_ref=src,
        dst_ref=dst,
        send_sem=ss,
        recv_sem=rs,
        device_id=device,
        device_id_type=MESH,
    )


def busy(half, device):
    return jnp.logical_and(device != IDLE[half][0], device != IDLE[half][1])


def spread_start(bufs, half, tm, back=False):
    src, dst, ss, rs = bufs

    def go(s, _):
        peer = lax.rem(tm + s, T)

        @pl.when(busy(half, tm if back else peer))
        def _():
            remote(
                src.at[half, peer], dst.at[half, tm], ss.at[half], rs.at[half], {"tm": peer}
            ).start()

        return 0

    lax.fori_loop(1, T, go, 0)
    dst[half, tm] = src[half, tm]


def spread_wait(bufs, half, tm, back=False):
    src, dst, ss, rs = bufs

    def chunks(count):
        some = pl.ds(0, count)
        return remote(
            src.at[half, some], dst.at[half, some], ss.at[half], rs.at[half],
            {"tm": lax.rem(tm + 1, T)},
        )

    working = busy(half, tm)

    @pl.when(working)
    def _():
        if back:
            chunks(31).wait_send()
            chunks(29).wait_recv()
        else:
            chunks(29).wait_send()
            chunks(31).wait_recv()

    @pl.when(jnp.logical_not(working))
    def _():
        if back:
            chunks(30).wait_recv()
        else:
            chunks(30).wait_send()
            dst[half] = jnp.zeros((T, PIX, C), BF16)


def spread_out(to, half, chunks):
    for device, first, count in RUNS[half]:
        to[half, device : device + count] = chunks[first : first + count]


def gathered(ref, half):
    runs = [ref[half, device : device + count] for device, _, count in RUNS[half]]
    return jnp.concatenate(runs, axis=0).reshape(30 * PIX, C)


def shifts(row):
    col = lax.broadcasted_iota(jnp.int32, (W, C), 0)
    before = jnp.where(col == 0, 0.0, pltpu.roll(row, 1, 0))
    after = jnp.where(col == W - 1, 0.0, pltpu.roll(row, W - 1, 0))
    return before, row, after


def fill(src, dst, first, count, forward):
    def go(i, _):
        before, here, after = shifts(src[i].astype(F32))
        parts = (before, here, after) if forward else (after, here, before)
        for b in range(3):
            dst[i, :, b * C : (b + 1) * C] = parts[b].astype(BF16)
        return 0

    lax.fori_loop(first, first + count, go, 0)


def taps(wide, start, count, forward):
    pieces = []
    for a in range(3):
        off = a if forward else 2 - a
        pieces.append(wide[start + off : start + off + count].reshape(count * W, 3 * C))
    return jnp.concatenate(pieces, axis=1)


def conv(wide, runs, weight, forward):
    lhs = [taps(wide, start, count, forward) for start, count in runs]
    lhs = lhs[0] if len(lhs) == 1 else jnp.concatenate(lhs, axis=0)
    out = jnp.dot(lhs, weight, preferred_element_type=F32)
    return out.reshape(out.shape[0] // W, W, C)


def nt(a, b):
    return lax.dot_general(a, b, (((1,), (1,)), ((), ())), preferred_element_type=F32)


def tn(a, b):
    return lax.dot_general(a, b, (((0,), (0,)), ((), ())), preferred_element_type=F32)


def attend(half, mt, gt, pt, aw, joined, work, unroll):
    stage, stage_g, mix, scale, qkv, ga, gup, normed, att, gj = work
    n = T * PIX
    base = half * n

    def widen(f, _):
        at = pl.ds(pl.multiple_of(f * PIX, PIX), PIX)
        for h in range(2):
            cols = pl.ds(h * 128, 128)
            stage[h, at, :] = mt[half, f, :, cols].astype(F32)
            stage_g[h, at, :] = gt[half, f, :, cols].astype(F32)
        return 0

    lax.fori_loop(0, T, widen, 0, unroll=4)

    def by_pixel(p, _):
        at = pl.ds(pl.multiple_of(p * T, T), T)
        to = pl.ds(pl.multiple_of(base + p * T, T), T)
        m = jnp.concatenate([stage[h, pl.ds(p, T, stride=PIX), :] for h in range(2)], axis=1)
        g = jnp.concatenate([stage_g[h, pl.ds(p, T, stride=PIX), :] for h in range(2)], axis=1)
        ns = lax.rsqrt(jnp.mean(m * m, axis=-1, keepdims=True) + EPSILON)
        mix[at, :] = m
        scale[at, :] = jnp.broadcast_to(ns, (T, 128))
        normed[to, :] = (m * ns).astype(BF16)
        gup[to, :] = g.astype(BF16)
        return 0

    lax.fori_loop(0, PIX, by_pixel, 0, unroll=4)
    every = pl.ds(base, n)
    qkv[...] = jnp.dot(normed[every, :], joined[...], preferred_element_type=F32).astype(BF16)
    ga[...] = nt(gup[every, :], aw[3]).astype(BF16)

    factor = 64.0**-0.5
    g = 128
    lane = lax.broadcasted_iota(jnp.int32, (1, C), 1) // 64
    head = [(lane == h).astype(F32).astype(BF16) for h in range(HEADS)]
    blocks = (
        lax.rem(lax.broadcasted_iota(jnp.int32, (HEADS * g, g), 0), g) // T
        == lax.broadcasted_iota(jnp.int32, (HEADS * g, g), 1) // T
    )

    def stack(x):
        return jnp.concatenate([x * head[h] for h in range(HEADS)], axis=0)

    def side(x):
        return jnp.concatenate([x[h * g : (h + 1) * g] for h in range(HEADS)], axis=1)

    def group(i, _):
        at = pl.ds(pl.multiple_of(i * g, g), g)
        to = pl.ds(pl.multiple_of(base + i * g, g), g)
        q, k, v = qkv[at, 0:C], qkv[at, C : 2 * C], qkv[at, 2 * C : 3 * C]
        qs, ks, vs, gas = stack(q), stack(k), stack(v), stack(ga[at, :])
        expo = jnp.where(blocks, jnp.exp(nt(qs, k) * factor), 0.0)
        probs = expo / jnp.sum(expo, axis=-1, keepdims=True)
        low = probs.astype(BF16)
        att[to, :] = jnp.dot(side(low), vs, preferred_element_type=F32).astype(BF16)
        gp = nt(gas, v)
        gs = probs * (gp - jnp.sum(probs * gp, axis=-1, keepdims=True))
        sl = (gs * factor).astype(BF16)
        gj[to, 0:C] = jnp.dot(side(sl), ks, preferred_element_type=F32).astype(BF16)
        gj[to, C : 2 * C] = tn(sl, qs).astype(BF16)
        gj[to, 2 * C : 3 * C] = tn(low, gas).astype(BF16)
        return 0

    lax.fori_loop(0, n // g, group, 0, unroll=unroll)
    step = 256
    for i in range(n // step):
        at = slice(i * step, (i + 1) * step)
        to = slice(base + i * step, base + (i + 1) * step)
        gn = nt(gj[to, :], joined[...])
        m = mix[at, :]
        ns = jnp.concatenate([scale[at, :]] * 2, axis=1)
        inner = jnp.mean(gn * m, axis=-1, keepdims=True)
        total = gup[to, :].astype(F32) + (ns * gn - m * ns * ns * ns * inner)
        for h in range(2):
            stage[h, at, :] = total[:, h * 128 : (h + 1) * 128]

    def by_frame(f, _):
        for h in range(2):
            pt[half, f, :, pl.ds(h * 128, 128)] = stage[h, pl.ds(f, PIX, stride=T), :].astype(BF16)
        return 0

    lax.fori_loop(0, T, by_frame, 0, unroll=4)


def attend_buffers():
    n = T * PIX
    return [
        pltpu.VMEM((2, n, 128), F32),
        pltpu.VMEM((2, n, 128), F32),
        pltpu.VMEM((n, C), F32),
        pltpu.VMEM((n, 128), F32),
        pltpu.VMEM((n, 3 * C), BF16),
        pltpu.VMEM((n, C), BF16),
        pltpu.VMEM((2 * n, C), BF16),
        pltpu.VMEM((2 * n, C), BF16),
        pltpu.VMEM((2 * n, C), BF16),
        pltpu.VMEM((2 * n, 3 * C), BF16),
    ]


class Reduction:
    @staticmethod
    def buffers(pairs, xp, joint):
        n, nx = pairs * 16, xp * 16
        ny = n - nx
        shapes = [
            *(() if joint else ((pairs, 2, 16, 16), (pairs, 16, 16))),
            (4, 4, nx), (4, 4, ny),
            (3, 4, nx), (3, 4, ny),
            (3, nx), (3, ny),
            (n,),
            (8, n),
            (n,),
        ]
        return [pltpu.VMEM(s + (C,), BF16) for s in shapes] + [dma(7 if joint else pairs + 7)] * 2

    def __init__(self, pairs, xp, joint, bufs, tm, rows):
        self.pairs, self.xp, self.joint = pairs, xp, joint
        self.skip = 0 if joint else pairs
        if not joint:
            self.packed, self.r1 = bufs[0:2]
            bufs = bufs[2:]
        self.n, self.nx = pairs * 16, xp * 16
        self.cut = self.nx
        self.ax1, self.ay1, self.rx2, self.ry2, self.rx3, self.ry3 = bufs[0:6]
        self.a3, self.r4, self.out, self.ss, self.rs = bufs[6:11]
        self.core, self.y, self.z_hi = lax.rem(tm, 2), lax.rem(tm // 2, 4), tm // 8
        self.x, self.z_lo = lax.rem(rows, 4), rows // 4
        self.tm, self.rows = tm, rows

    def copy(self, src, dst, s, r, device):
        return remote(
            src, dst, self.ss.at[self.skip + s], self.rs.at[self.skip + r], device
        )

    def tm_at(self, z_hi, y):
        return {"tm": z_hi * 8 + y * 2 + self.core}

    def row_at(self, z_lo, x):
        return {"rows": z_lo * 4 + x}

    def first(self, j):
        other = {"tm": self.tm + 1 - 2 * self.core}
        return remote(
            self.packed.at[j, 1 - self.core], self.r1.at[j], self.ss.at[j], self.rs.at[j], other
        )

    def place(self, j):
        in_x = j < self.xp
        return self.ax1 if in_x else self.ay1, pl.ds((j if in_x else j - self.xp) * 16, 16)

    def send_on(self, j):
        if j == self.xp - 1 or j == self.pairs - 1:
            for s in (1, 2, 3):
                (self.second_x if j < self.xp else self.second_y)(s).start()

    def send(self, j, upper, lower):
        for t in range(T // 2 if self.joint else T):
            both = jnp.concatenate([upper[t * 8 : t * 8 + 8], lower[t * 8 : t * 8 + 8]], axis=0)
            core, t = (0, t) if self.joint else (t % 2, t // 2)
            z, y = t // 4, t % 4
            k = z * 4 + y if j < self.xp else y * 4 + z
            if self.joint:
                to, at = self.place(j)
                to[k // 4, k % 4, at, :] = both.astype(BF16)
            else:
                self.packed[j, core, k] = both.astype(BF16)
        if self.joint:
            self.send_on(j)
        else:
            self.first(j).start()

    def second_x(self, s):
        x = lax.rem(self.x + s, 4)
        return self.copy(self.ax1.at[x], self.rx2.at[s - 1], 0, 0, self.row_at(self.z_lo, x))

    def second_y(self, s):
        y = lax.rem(self.y + s, 4)
        return self.copy(self.ay1.at[y], self.ry2.at[s - 1], 1, 1, self.tm_at(self.z_hi, y))

    def third_x(self, s):
        y = lax.rem(self.y + s, 4)
        return self.copy(
            self.ax1.at[self.x, y], self.rx3.at[s - 1], 2, 2, self.tm_at(self.z_hi, y)
        )

    def third_y(self, s):
        x = lax.rem(self.x + s, 4)
        return self.copy(
            self.ay1.at[self.y, x], self.ry3.at[s - 1], 3, 3, self.row_at(self.z_lo, x)
        )

    def piece(self, k):
        return pl.ds(0, self.cut) if k == 0 else pl.ds(self.cut, self.n - self.cut)

    def fourth(self, k):
        z = self.z_hi * 2 + self.z_lo
        at = self.piece(k)
        device = {"tm": self.x * 8 + self.y * 2 + self.core, "rows": k * 4 + self.x}
        return self.copy(self.a3.at[at], self.r4.at[z, at], 4 + k, 4, device)

    def fifth(self, k, s):
        at = self.piece(k)
        peer = lax.rem(self.rows + s, R)
        return self.copy(self.out.at[at], self.out.at[at], 6, 5 + k, {"rows": peer})

    def wait(self, src, dst, s, r, send=True, recv=True):
        copy = self.copy(src, dst, s, r, {"rows": lax.rem(self.rows + 1, R)})
        if send:
            copy.wait_send()
        if recv:
            copy.wait_recv()

    def holds(self, k):
        return jnp.logical_and(self.z_hi == self.x, self.z_lo == k)

    def away(self, k):
        return jnp.logical_not(self.holds(k))

    def after_core(self):
        for j in range(self.pairs):
            self.first(j).wait()
            to, at = self.place(j)
            total = self.packed[j, self.core].astype(F32) + self.r1[j].astype(F32)
            to[:, :, at, :] = total.astype(BF16).reshape(4, 4, 16, C)
            self.send_on(j)

    def after_second(self):
        for a, r, me, i, go in (
            (self.ax1, self.rx2, self.x, 0, self.third_x),
            (self.ay1, self.ry2, self.y, 1, self.third_y),
        ):
            self.wait(r, r, i, i)
            total = a[me].astype(F32)
            for s in range(3):
                total += r[s].astype(F32)
            a[me] = total.astype(BF16)
            for s in (1, 2, 3):
                go(s).start()

    def after_third(self):
        for a, r, i, j, at, sem in (
            (self.ax1, self.rx3, self.x, self.y, pl.ds(0, self.nx), 2),
            (self.ay1, self.ry3, self.y, self.x, pl.ds(self.nx, self.n - self.nx), 3),
        ):
            self.wait(r, r, sem, sem)
            total = a[i, j].astype(F32)
            for s in range(3):
                total += r[s].astype(F32)
            self.a3[at, :] = total.astype(BF16)
        for k in range(2):

            @pl.when(self.away(k))
            def _():
                self.fourth(k).start()

    def after_fourth(self):
        for k in range(2):

            @pl.when(self.away(k))
            def _():
                self.fourth(k).wait_send()

            @pl.when(self.holds(k))
            def _():
                at = self.piece(k)
                mine = self.z_hi * 2 + k
                seven = self.r4.at[pl.ds(0, 7), at]
                self.wait(seven, seven, 4, 4, send=False)
                self.r4[mine, at, :] = self.a3[at, :]
                total = self.r4[0, at, :].astype(F32)
                for z in range(1, 8):
                    total += self.r4[z, at, :].astype(F32)
                self.out[at, :] = total.astype(BF16)
                for s in range(1, R):
                    self.fifth(k, s).start()

    def finish(self):
        for k in range(2):

            @pl.when(self.holds(k))
            def _():
                seven = self.r4.at[pl.ds(0, 7), self.piece(k)]
                self.wait(seven, seven, 6, 5 + k, recv=False)

            @pl.when(self.away(k))
            def _():
                self.fifth(k, 1).wait_recv()

        return self.out[...].astype(F32) * (float(T * NR * R * W) ** -0.5)


def zero_at(ref, where, condition):
    @pl.when(condition)
    def _():
        ref[where] = jnp.zeros(ref[where].shape, ref.dtype)


def block_kernel(
    x_hbm, g_hbm, w_hbm, aw_hbm,
    dx, dconv, dattn,
    xe, ae, hid, w_ref, kt, aw, joined, gpad, gt, mpad, mt, pt, gm,
    xc, ac, ge, uc, pre, pc, g1, xt, at0, at1, xs, as0, as1, u0, s0, u1, s1,
    gs, gr, ms, mr, ps, pr, hs, hr, ks, kr, ls, ts, tr,
    *bufs,
):
    tm, rows = lax.axis_index("tm"), lax.axis_index("rows")
    up = {"rows": lax.rem(rows + R - 1, R)}
    down = {"rows": lax.rem(rows + 1, R)}
    top, bottom = rows == 0, rows == R - 1
    work, bufs = bufs[:10], bufs[10:]
    attn = Reduction(2, 1, False, bufs[:13], tm, rows)
    early = Reduction(4, 2, True, bufs[13:24], tm, rows)
    late = Reduction(5, 3, True, bufs[24:], tm, rows)
    core = lax.rem(tm, 2)
    twin = {"tm": tm + 1 - 2 * core}
    g_bufs, m_bufs, p_bufs = (gpad, gt, gs, gr), (mpad, mt, ms, mr), (pt, gm, ps, pr)

    loads = [
        pltpu.make_async_copy(x_hbm, xe.at[pl.ds(2, NR)], ls.at[0]),
        *(
            pltpu.make_async_copy(
                g_hbm.at[pl.ds(first, count)], gpad.at[half, pl.ds(device, count)], ls.at[1 + k]
            )
            for k, (half, device, first, count) in enumerate(
                ((0, 1, 0, 9), (0, 11, 9, 1), (0, 12, 40, 20), (1, 0, 10, 20), (1, 21, 30, 9), (1, 31, 39, 1))
            )
        ),
        pltpu.make_async_copy(w_hbm, w_ref, ls.at[7]),
        pltpu.make_async_copy(aw_hbm, aw, ls.at[8]),
    ]
    for load in loads:
        load.start()
    for half in range(2):
        for device in IDLE[half]:
            gpad[half, device] = jnp.zeros((PIX, C), BF16)
            mpad[half, device] = jnp.zeros((PIX, C), BF16)
    barrier(tm, rows)
    loads[0].wait()
    to_up = remote(xe.at[pl.ds(2, 2)], xe.at[pl.ds(NR + 2, 2)], hs.at[0], hr.at[0], up)
    to_down = remote(xe.at[pl.ds(NR, 2)], xe.at[pl.ds(0, 2)], hs.at[1], hr.at[1], down)
    to_up.start()
    to_down.start()
    for load in loads[1:7]:
        load.wait()
    spread_start(g_bufs, 0, tm)
    fill(xe, xc, 2, NR, True)

    def keep(first, hidden):
        hid[first : first + hidden.shape[0]] = hidden
        ae[first : first + hidden.shape[0]] = (hidden * jax.nn.sigmoid(hidden)).astype(BF16)

    loads[7].wait()
    keep(2, conv(xc, ((2, 4),), w_ref[0], True))
    spread_start(g_bufs, 1, tm)
    to_up.wait()
    to_down.wait()
    zero_at(xe, slice(0, 2), top)
    zero_at(xe, slice(NR + 2, NR + 4), bottom)
    fill(xe, xc, 0, 2, True)
    fill(xe, xc, NR + 2, 2, True)
    ends = conv(xc, ((0, 2), (6, 2)), w_ref[0], True)
    keep(0, ends[0:2])
    keep(6, ends[2:4])
    zero_at(ae, slice(0, 1), top)
    zero_at(ae, slice(NR + 1, NR + 2), bottom)
    fill(ae, ac, 0, NR + 2, True)
    branch = conv(ac, ((0, 1), (4, 2)), w_ref[1], True)
    mixed = jnp.concatenate([xe[2:3], xe[6:8]], axis=0).astype(F32) + branch
    spread_out(mpad, 0, mixed.astype(BF16).reshape(30, PIX, C))
    spread_start(m_bufs, 0, tm)
    mixed = xe[3:6].astype(F32) + conv(ac, ((1, 3),), w_ref[1], True)
    spread_out(mpad, 1, mixed.astype(BF16).reshape(30, PIX, C))
    spread_wait(g_bufs, 0, tm)
    loads[8].wait()
    joined[...] = jnp.concatenate([aw[0], aw[1], aw[2]], axis=1)

    def turn(i, _):
        for k in range(2):
            at = pl.ds(pl.multiple_of(i * C, C), C)
            kt[k, at, :] = w_ref[k, at, :].astype(F32).T.astype(BF16)
        return 0

    lax.fori_loop(0, 9, turn, 0)

    def slopes(i, _):
        h = hid[i]
        s = jax.nn.sigmoid(h)
        hid[i] = s * (1.0 + h * (1.0 - s))
        return 0

    lax.fori_loop(0, NR + 2, slopes, 0)

    def flip(to, a, b, pieces, depth):
        rows_in = [p.reshape(-1, C).astype(F32) for p in pieces]
        short = depth - sum(p.shape[0] for p in rows_in)
        flat = jnp.concatenate(rows_in + [jnp.zeros((short, C), F32)], axis=0).T
        flat = flat.reshape(16, 2, 8, depth)
        for c in range(2):
            to[c, a, b * 128 : (b + 1) * 128, :] = flat[:, c].reshape(128, depth).astype(BF16)

    def flips(a, _):
        for b in range(3):
            at = pl.ds(b * C, C)
            flip(xt, a, b, [xc[pl.ds(a + 1, NR), :, at]], 1024)
            flip(at0, a, b, [ac[pl.ds(a, 1), :, at], ac[pl.ds(a + 4, 2), :, at]], 512)
            flip(at1, a, b, [ac[pl.ds(a + 1, 3), :, at]], 512)
        return 0

    lax.fori_loop(0, 3, flips, 0)
    swaps = [
        remote(src.at[1 - core], dst, ts.at[k], tr.at[k], twin)
        for k, (src, dst) in enumerate(((at0, as0), (at1, as1), (xt, xs)))
    ]
    for swap in swaps:
        swap.start()
    for buf in (u1, s1):
        buf[:, 480:512] = jnp.zeros((2, 32, C), BF16)
    for buf in (u0, s0):
        buf[960:1024] = jnp.zeros((64, C), BF16)
    full = pl.ds(0, 480)
    u_swaps = [
        remote(u1.at[0, full], s1.at[0, full], ts.at[3], tr.at[3], twin),
        remote(u1.at[1, full], s1.at[1, full], ts.at[4], tr.at[4], twin),
        remote(u0.at[pl.ds(0, 960)], s0.at[pl.ds(0, 960)], ts.at[5], tr.at[5], twin),
    ]
    spread_wait(g_bufs, 1, tm)
    spread_start(m_bufs, 1, tm)
    for half in range(2):
        spread_wait(m_bufs, half, tm)
        attend(half, mt, gt, pt, aw, joined, work, UNROLL)
        spread_start(p_bufs, half, tm, True)

    gup, normed, att, gj = work[6:10]
    proj = tn(normed[...], gj[...])
    attn.send(0, proj[:, 0:C], proj[:, C : 2 * C])
    attn.send(1, proj[:, 2 * C : 3 * C], tn(att[...], gup[...]))

    spread_wait(p_bufs, 0, tm, True)
    outer = gathered(gm, 0)
    ge[2:3] = outer[0:W].reshape(1, W, C)
    ge[6:8] = outer[W:].reshape(2, W, C)
    u1[0, 0:480] = outer
    u_swaps[0].start()
    near_up = remote(ge.at[2], ge.at[NR + 2], ks.at[0], kr.at[0], up)
    near_down = remote(ge.at[NR + 1], ge.at[1], ks.at[1], kr.at[1], down)
    near_up.start()
    near_down.start()
    fill(ge, uc, 2, 1, False)
    fill(ge, uc, 6, 2, False)

    def times(a, b):
        return jnp.dot(a, b, preferred_element_type=F32)

    for swap in swaps:
        swap.wait()
    u_swaps[0].wait()
    for a in range(3):
        g1[a] = times(at0[core, a], u1[0]) + times(as0[a], s1[0])
    attn.after_core()

    def one(k):
        return g1[k // 3, (k % 3) * 128 : (k % 3 + 1) * 128, :]

    spread_wait(p_bufs, 1, tm, True)
    inner = gathered(gm, 1)
    ge[3:6] = inner.reshape(3, W, C)
    u1[1, 0:480] = inner
    u_swaps[1].start()
    far_up = remote(ge.at[3], ge.at[NR + 3], ks.at[2], kr.at[2], up)
    far_down = remote(ge.at[NR], ge.at[0], ks.at[3], kr.at[3], down)
    far_up.start()
    far_down.start()
    fill(ge, uc, 3, 3, False)

    def back(first, act_grad):
        at = slice(first, first + act_grad.shape[0])
        pre[at] = (act_grad.astype(BF16).astype(F32) * hid[at]).astype(BF16)

    near_up.wait()
    near_down.wait()
    zero_at(ge, slice(1, 2), top)
    zero_at(ge, slice(NR + 2, NR + 3), bottom)
    fill(ge, uc, 1, 1, False)
    fill(ge, uc, NR + 2, 1, False)
    back(1, conv(uc, ((1, 6),), kt[1], False))
    u0[0:960] = pre[1 : NR + 1].reshape(960, C)
    u_swaps[2].start()
    u_swaps[1].wait()
    for a in range(3):
        g1[a] += times(at1[core, a], u1[1]) + times(as1[a], s1[1])
        for j in ((0,), (1, 2), (3,))[a]:
            early.send(j, one(2 * j), one(2 * j + 1))
    g0 = []

    def zero(k):
        return g0[k // 3][(k % 3) * 128 : (k % 3 + 1) * 128]

    u_swaps[2].wait()
    for a in range(3):
        g0.append(times(xt[core, a], u0[...]) + times(xs[a], s0[...]))
        for j in ((0,), (1, 2), (3, 4))[a]:
            late.send(j, zero(2 * j), zero(2 * j + 1) if j < 4 else one(8))
    attn.after_second()
    far_up.wait()
    far_down.wait()
    zero_at(ge, slice(0, 1), top)
    zero_at(ge, slice(NR + 3, NR + 4), bottom)
    fill(ge, uc, 0, 1, False)
    fill(ge, uc, NR + 3, 1, False)
    ends = conv(uc, ((0, 1), (7, 1)), kt[1], False)
    back(0, ends[0:1])
    back(7, ends[1:2])
    zero_at(pre, slice(0, 1), top)
    zero_at(pre, slice(NR + 1, NR + 2), bottom)
    fill(pre, pc, 0, NR + 2, False)
    early.after_second()
    dx[...] = (ge[2:8].astype(F32) + conv(pc, ((0, 6),), kt[0], False)).astype(BF16)
    attn.after_third()
    late.after_second()
    early.after_third()
    late.after_third()
    attn.after_fourth()
    early.after_fourth()
    late.after_fourth()
    dattn[...] = attn.finish().reshape(4, 8, C)
    dconv[1, 0:8] = early.finish().reshape(8, 8, C)
    sums = late.finish()
    dconv[0] = sums[0:72].reshape(9, 8, C)
    dconv[1, 8:9] = sums[72:80].reshape(1, 8, C)


def pass_kernel(a, b, c, x, y, z, va, vb, vc, sems):
    trips = [(a.at[i], va.at[i], x.at[i]) for i in range(NR)] + [(b, vb, y), (c, vc, z)]
    into = [pltpu.make_async_copy(s, v, sems.at[k]) for k, (s, v, _) in enumerate(trips)]
    out = [pltpu.make_async_copy(v, d, sems.at[8 + k]) for k, (_, v, d) in enumerate(trips)]
    for copy in into:
        copy.start()
    for k in range(8):
        into[k].wait()
        out[k].start()
    for copy in out:
        copy.wait()


def anywhere(count):
    return [pl.BlockSpec(memory_space=pl.ANY)] * count


def vmem(count):
    return [pl.BlockSpec(memory_space=pltpu.VMEM)] * count


def dma(*shape):
    return pltpu.SemaphoreType.DMA(shape)


def params(collective_id=None):
    if collective_id is None:
        return pltpu.CompilerParams(vmem_limit_bytes=VMEM_LIMIT)
    return pltpu.CompilerParams(
        vmem_limit_bytes=VMEM_LIMIT, collective_id=collective_id, has_side_effects=True
    )


def per_device(frames_in, grad_out, conv_weight, attn_weight):
    x = frames_in.reshape(NR, W, C)
    g = grad_out.reshape(NR * W // PIX, PIX, C)
    w = conv_weight.reshape(2, 9 * C, C)
    spread = pltpu.VMEM((2, T, PIX, C), BF16)
    shapes = [
        jax.ShapeDtypeStruct((NR, W, C), BF16),
        jax.ShapeDtypeStruct((2, 9, 8, C), F32),
        jax.ShapeDtypeStruct((4, 8, C), F32),
    ]
    outs = pl.pallas_call(
        block_kernel,
        out_shape=shapes,
        in_specs=anywhere(4),
        out_specs=vmem(3),
        scratch_shapes=[
            pltpu.VMEM((NR + 4, W, C), BF16),
            pltpu.VMEM((NR + 2, W, C), BF16),
            pltpu.VMEM((NR + 2, W, C), F32),
            pltpu.VMEM((2, 9 * C, C), BF16),
            pltpu.VMEM((2, 9 * C, C), BF16),
            pltpu.VMEM((4, C, C), BF16),
            pltpu.VMEM((C, 3 * C), BF16),
            *[spread] * 6,
            pltpu.VMEM((NR + 4, W, 3 * C), BF16),
            pltpu.VMEM((NR + 2, W, 3 * C), BF16),
            pltpu.VMEM((NR + 4, W, C), BF16),
            pltpu.VMEM((NR + 4, W, 3 * C), BF16),
            pltpu.VMEM((NR + 2, W, C), BF16),
            pltpu.VMEM((NR + 2, W, 3 * C), BF16),
            pltpu.VMEM((3, 384, C), F32),
            pltpu.VMEM((2, 3, 384, 1024), BF16),
            pltpu.VMEM((2, 3, 384, 512), BF16),
            pltpu.VMEM((2, 3, 384, 512), BF16),
            pltpu.VMEM((3, 384, 1024), BF16),
            pltpu.VMEM((3, 384, 512), BF16),
            pltpu.VMEM((3, 384, 512), BF16),
            pltpu.VMEM((1024, C), BF16),
            pltpu.VMEM((1024, C), BF16),
            pltpu.VMEM((2, 512, C), BF16),
            pltpu.VMEM((2, 512, C), BF16),
            *[dma(2)] * 6,
            dma(2), dma(2), dma(4), dma(4), dma(9), dma(6), dma(6),
            *attend_buffers(),
            *Reduction.buffers(2, 1, False),
            *Reduction.buffers(4, 2, True),
            *Reduction.buffers(5, 3, True),
        ],
        compiler_params=params(1),
        name="block",
    )(x, g, w, attn_weight)
    dx, dconv, dattn = pl.pallas_call(
        pass_kernel,
        out_shape=shapes,
        in_specs=anywhere(3),
        out_specs=anywhere(3),
        scratch_shapes=[*[pltpu.VMEM(s.shape, s.dtype) for s in shapes], dma(16)],
        compiler_params=params(),
        name="hand_on",
    )(*outs)
    return dx.reshape(1, NR, W, C), dconv, dattn


def solution(mesh):
    return jax.shard_map(
        per_device,
        mesh=mesh,
        in_specs=(P("tm", "rows", None, None), P("tm", "rows", None, None), P(), P()),
        out_specs=(P("tm", "rows", None, None), P(None, None, "tm", None), P(None, "tm", None)),
        check_vma=False,
    )
```

```python
import functools

import jax
import jax.numpy as jnp
from jax import lax
from jax.experimental import pallas as pl
from jax.experimental.pallas import tpu as pltpu
from jax.sharding import PartitionSpec as P

HEADS = 4
EPSILON = 1e-06
T, R = 32, 8
NR, W, C = 6, 160, 256
PIX = 16
UNROLL = 4
IDLE = ((0, 10), (20, 30))
RUNS = (((1, 0, 9), (11, 9, 21)), ((0, 0, 20), (21, 20, 9), (31, 29, 1)))
F32, BF16 = jnp.float32, jnp.bfloat16
MESH = pl.DeviceIdType.MESH
VMEM_LIMIT = 60 * 1024 * 1024


def signal(sem, device):
    pl.semaphore_signal(sem, inc=1, device_id=device, device_id_type=MESH)


def barrier(tm, rows):
    sem = pltpu.get_barrier_semaphore()

    def tell_tm(s, _):
        signal(sem, {"tm": lax.rem(tm + s, T)})
        return 0

    lax.fori_loop(1, T, tell_tm, 0)
    for s in range(1, R):
        signal(sem, {"rows": lax.rem(rows + s, R)})
    for s in (8, 16, 24):
        signal(sem, {"tm": lax.rem(tm + s, T), "rows": lax.rem(rows + 4, R)})
    pl.semaphore_wait(sem, T - 1 + R - 1 + 3)


def remote(src, dst, ss, rs, device):
    return pltpu.make_async_remote_copy(
        src_ref=src,
        dst_ref=dst,
        send_sem=ss,
        recv_sem=rs,
        device_id=device,
        device_id_type=MESH,
    )


def busy(half, device):
    return jnp.logical_and(device != IDLE[half][0], device != IDLE[half][1])


def spread_start(bufs, half, tm, back=False):
    src, dst, ss, rs = bufs

    def go(s, _):
        peer = lax.rem(tm + s, T)

        @pl.when(busy(half, tm if back else peer))
        def _():
            remote(
                src.at[half, peer], dst.at[half, tm], ss.at[half], rs.at[half], {"tm": peer}
            ).start()

        return 0

    lax.fori_loop(1, T, go, 0)
    dst[half, tm] = src[half, tm]


def spread_wait(bufs, half, tm, back=False):
    src, dst, ss, rs = bufs

    def chunks(count):
        some = pl.ds(0, count)
        return remote(
            src.at[half, some], dst.at[half, some], ss.at[half], rs.at[half],
            {"tm": lax.rem(tm + 1, T)},
        )

    working = busy(half, tm)

    @pl.when(working)
    def _():
        if back:
            chunks(31).wait_send()
            chunks(29).wait_recv()
        else:
            chunks(29).wait_send()
            chunks(31).wait_recv()

    @pl.when(jnp.logical_not(working))
    def _():
        if back:
            chunks(30).wait_recv()
        else:
            chunks(30).wait_send()
            dst[half] = jnp.zeros((T, PIX, C), BF16)


def spread_out(to, half, chunks):
    for device, first, count in RUNS[half]:
        to[half, device : device + count] = chunks[first : first + count]


def gathered(ref, half):
    runs = [ref[half, device : device + count] for device, _, count in RUNS[half]]
    return jnp.concatenate(runs, axis=0).reshape(30 * PIX, C)


def shifts(row):
    col = lax.broadcasted_iota(jnp.int32, (W, C), 0)
    before = jnp.where(col == 0, 0.0, pltpu.roll(row, 1, 0))
    after = jnp.where(col == W - 1, 0.0, pltpu.roll(row, W - 1, 0))
    return before, row, after


def fill(src, dst, first, count, forward):
    def go(i, _):
        before, here, after = shifts(src[i].astype(F32))
        parts = (before, here, after) if forward else (after, here, before)
        for b in range(3):
            dst[i, :, b * C : (b + 1) * C] = parts[b].astype(BF16)
        return 0

    lax.fori_loop(first, first + count, go, 0)


def taps(wide, start, count, forward):
    pieces = []
    for a in range(3):
        off = a if forward else 2 - a
        pieces.append(wide[start + off : start + off + count].reshape(count * W, 3 * C))
    return jnp.concatenate(pieces, axis=1)


def conv(wide, runs, weight, forward):
    lhs = [taps(wide, start, count, forward) for start, count in runs]
    lhs = lhs[0] if len(lhs) == 1 else jnp.concatenate(lhs, axis=0)
    out = jnp.dot(lhs, weight, preferred_element_type=F32)
    return out.reshape(out.shape[0] // W, W, C)


def nt(a, b):
    return lax.dot_general(a, b, (((1,), (1,)), ((), ())), preferred_element_type=F32)


def tn(a, b):
    return lax.dot_general(a, b, (((0,), (0,)), ((), ())), preferred_element_type=F32)


def attend(half, mt, gt, pt, aw, joined, work, unroll):
    stage, stage_g, mix, scale, qkv, ga, gup, normed, att, gj = work
    n = T * PIX
    base = half * n

    def widen(f, _):
        at = pl.ds(pl.multiple_of(f * PIX, PIX), PIX)
        for h in range(2):
            cols = pl.ds(h * 128, 128)
            stage[h, at, :] = mt[half, f, :, cols].astype(F32)
            stage_g[h, at, :] = gt[half, f, :, cols].astype(F32)
        return 0

    lax.fori_loop(0, T, widen, 0, unroll=4)

    def by_pixel(p, _):
        at = pl.ds(pl.multiple_of(p * T, T), T)
        to = pl.ds(pl.multiple_of(base + p * T, T), T)
        m = jnp.concatenate([stage[h, pl.ds(p, T, stride=PIX), :] for h in range(2)], axis=1)
        g = jnp.concatenate([stage_g[h, pl.ds(p, T, stride=PIX), :] for h in range(2)], axis=1)
        ns = lax.rsqrt(jnp.mean(m * m, axis=-1, keepdims=True) + EPSILON)
        mix[at, :] = m
        scale[at, :] = jnp.broadcast_to(ns, (T, 128))
        normed[to, :] = (m * ns).astype(BF16)
        gup[to, :] = g.astype(BF16)
        return 0

    lax.fori_loop(0, PIX, by_pixel, 0, unroll=4)
    every = pl.ds(base, n)
    qkv[...] = jnp.dot(normed[every, :], joined[...], preferred_element_type=F32).astype(BF16)
    ga[...] = nt(gup[every, :], aw[3]).astype(BF16)

    factor = 64.0**-0.5
    g = 128
    lane = lax.broadcasted_iota(jnp.int32, (1, C), 1) // 64
    head = [(lane == h).astype(F32).astype(BF16) for h in range(HEADS)]
    blocks = (
        lax.rem(lax.broadcasted_iota(jnp.int32, (HEADS * g, g), 0), g) // T
        == lax.broadcasted_iota(jnp.int32, (HEADS * g, g), 1) // T
    )

    def stack(x):
        return jnp.concatenate([x * head[h] for h in range(HEADS)], axis=0)

    def side(x):
        return jnp.concatenate([x[h * g : (h + 1) * g] for h in range(HEADS)], axis=1)

    def group(i, _):
        at = pl.ds(pl.multiple_of(i * g, g), g)
        to = pl.ds(pl.multiple_of(base + i * g, g), g)
        q, k, v = qkv[at, 0:C], qkv[at, C : 2 * C], qkv[at, 2 * C : 3 * C]
        qs, ks, vs, gas = stack(q), stack(k), stack(v), stack(ga[at, :])
        expo = jnp.where(blocks, jnp.exp(nt(qs, k) * factor), 0.0)
        probs = expo / jnp.sum(expo, axis=-1, keepdims=True)
        low = probs.astype(BF16)
        att[to, :] = jnp.dot(side(low), vs, preferred_element_type=F32).astype(BF16)
        gp = nt(gas, v)
        gs = probs * (gp - jnp.sum(probs * gp, axis=-1, keepdims=True))
        sl = (gs * factor).astype(BF16)
        gj[to, 0:C] = jnp.dot(side(sl), ks, preferred_element_type=F32).astype(BF16)
        gj[to, C : 2 * C] = tn(sl, qs).astype(BF16)
        gj[to, 2 * C : 3 * C] = tn(low, gas).astype(BF16)
        return 0

    lax.fori_loop(0, n // g, group, 0, unroll=unroll)
    step = 256
    for i in range(n // step):
        at = slice(i * step, (i + 1) * step)
        to = slice(base + i * step, base + (i + 1) * step)
        gn = nt(gj[to, :], joined[...])
        m = mix[at, :]
        ns = jnp.concatenate([scale[at, :]] * 2, axis=1)
        inner = jnp.mean(gn * m, axis=-1, keepdims=True)
        total = gup[to, :].astype(F32) + (ns * gn - m * ns * ns * ns * inner)
        for h in range(2):
            stage[h, at, :] = total[:, h * 128 : (h + 1) * 128]

    def by_frame(f, _):
        for h in range(2):
            pt[half, f, :, pl.ds(h * 128, 128)] = stage[h, pl.ds(f, PIX, stride=T), :].astype(BF16)
        return 0

    lax.fori_loop(0, T, by_frame, 0, unroll=4)


def attend_buffers():
    n = T * PIX
    return [
        pltpu.VMEM((2, n, 128), F32),
        pltpu.VMEM((2, n, 128), F32),
        pltpu.VMEM((n, C), F32),
        pltpu.VMEM((n, 128), F32),
        pltpu.VMEM((n, 3 * C), BF16),
        pltpu.VMEM((n, C), BF16),
        pltpu.VMEM((2 * n, C), BF16),
        pltpu.VMEM((2 * n, C), BF16),
        pltpu.VMEM((2 * n, C), BF16),
        pltpu.VMEM((2 * n, 3 * C), BF16),
    ]


class Reduction:
    @staticmethod
    def buffers(pairs, xp, joint):
        n, nx = pairs * 16, xp * 16
        ny = n - nx
        shapes = [
            *(() if joint else ((pairs, 2, 16, 16), (pairs, 16, 16))),
            (4, 4, nx), (4, 4, ny),
            (3, 4, nx), (3, 4, ny),
            (3, nx), (3, ny),
            (n,),
            (8, n),
            (n,),
        ]
        return [pltpu.VMEM(s + (C,), BF16) for s in shapes] + [dma(7 if joint else pairs + 7)] * 2

    def __init__(self, pairs, xp, joint, bufs, tm, rows):
        self.pairs, self.xp, self.joint = pairs, xp, joint
        self.skip = 0 if joint else pairs
        if not joint:
            self.packed, self.r1 = bufs[0:2]
            bufs = bufs[2:]
        self.n, self.nx = pairs * 16, xp * 16
        self.cut = self.nx
        self.ax1, self.ay1, self.rx2, self.ry2, self.rx3, self.ry3 = bufs[0:6]
        self.a3, self.r4, self.out, self.ss, self.rs = bufs[6:11]
        self.core, self.y, self.z_hi = lax.rem(tm, 2), lax.rem(tm // 2, 4), tm // 8
        self.x, self.z_lo = lax.rem(rows, 4), rows // 4
        self.tm, self.rows = tm, rows

    def copy(self, src, dst, s, r, device):
        return remote(
            src, dst, self.ss.at[self.skip + s], self.rs.at[self.skip + r], device
        )

    def tm_at(self, z_hi, y):
        return {"tm": z_hi * 8 + y * 2 + self.core}

    def row_at(self, z_lo, x):
        return {"rows": z_lo * 4 + x}

    def first(self, j):
        other = {"tm": self.tm + 1 - 2 * self.core}
        return remote(
            self.packed.at[j, 1 - self.core], self.r1.at[j], self.ss.at[j], self.rs.at[j], other
        )

    def place(self, j):
        in_x = j < self.xp
        return self.ax1 if in_x else self.ay1, pl.ds((j if in_x else j - self.xp) * 16, 16)

    def send_on(self, j):
        if j == self.xp - 1 or j == self.pairs - 1:
            for s in (1, 2, 3):
                (self.second_x if j < self.xp else self.second_y)(s).start()

    def send(self, j, upper, lower):
        for t in range(T // 2 if self.joint else T):
            both = jnp.concatenate([upper[t * 8 : t * 8 + 8], lower[t * 8 : t * 8 + 8]], axis=0)
            core, t = (0, t) if self.joint else (t % 2, t // 2)
            z, y = t // 4, t % 4
            k = z * 4 + y if j < self.xp else y * 4 + z
            if self.joint:
                to, at = self.place(j)
                to[k // 4, k % 4, at, :] = both.astype(BF16)
            else:
                self.packed[j, core, k] = both.astype(BF16)
        if self.joint:
            self.send_on(j)
        else:
            self.first(j).start()

    def second_x(self, s):
        x = lax.rem(self.x + s, 4)
        return self.copy(self.ax1.at[x], self.rx2.at[s - 1], 0, 0, self.row_at(self.z_lo, x))

    def second_y(self, s):
        y = lax.rem(self.y + s, 4)
        return self.copy(self.ay1.at[y], self.ry2.at[s - 1], 1, 1, self.tm_at(self.z_hi, y))

    def third_x(self, s):
        y = lax.rem(self.y + s, 4)
        return self.copy(
            self.ax1.at[self.x, y], self.rx3.at[s - 1], 2, 2, self.tm_at(self.z_hi, y)
        )

    def third_y(self, s):
        x = lax.rem(self.x + s, 4)
        return self.copy(
            self.ay1.at[self.y, x], self.ry3.at[s - 1], 3, 3, self.row_at(self.z_lo, x)
        )

    def piece(self, k):
        return pl.ds(0, self.cut) if k == 0 else pl.ds(self.cut, self.n - self.cut)

    def fourth(self, k):
        z = self.z_hi * 2 + self.z_lo
        at = self.piece(k)
        device = {"tm": self.x * 8 + self.y * 2 + self.core, "rows": k * 4 + self.x}
        return self.copy(self.a3.at[at], self.r4.at[z, at], 4 + k, 4, device)

    def fifth(self, k, s):
        at = self.piece(k)
        peer = lax.rem(self.rows + s, R)
        return self.copy(self.out.at[at], self.out.at[at], 6, 5 + k, {"rows": peer})

    def wait(self, src, dst, s, r, send=True, recv=True):
        copy = self.copy(src, dst, s, r, {"rows": lax.rem(self.rows + 1, R)})
        if send:
            copy.wait_send()
        if recv:
            copy.wait_recv()

    def holds(self, k):
        return jnp.logical_and(self.z_hi == self.x, self.z_lo == k)

    def away(self, k):
        return jnp.logical_not(self.holds(k))

    def after_core(self):
        for j in range(self.pairs):
            self.first(j).wait()
            to, at = self.place(j)
            total = self.packed[j, self.core].astype(F32) + self.r1[j].astype(F32)
            to[:, :, at, :] = total.astype(BF16).reshape(4, 4, 16, C)
            self.send_on(j)

    def after_second(self):
        for a, r, me, i, go in (
            (self.ax1, self.rx2, self.x, 0, self.third_x),
            (self.ay1, self.ry2, self.y, 1, self.third_y),
        ):
            self.wait(r, r, i, i)
            total = a[me].astype(F32)
            for s in range(3):
                total += r[s].astype(F32)
            a[me] = total.astype(BF16)
            for s in (1, 2, 3):
                go(s).start()

    def after_third(self):
        for a, r, i, j, at, sem in (
            (self.ax1, self.rx3, self.x, self.y, pl.ds(0, self.nx), 2),
            (self.ay1, self.ry3, self.y, self.x, pl.ds(self.nx, self.n - self.nx), 3),
        ):
            self.wait(r, r, sem, sem)
            total = a[i, j].astype(F32)
            for s in range(3):
                total += r[s].astype(F32)
            self.a3[at, :] = total.astype(BF16)
        for k in range(2):

            @pl.when(self.away(k))
            def _():
                self.fourth(k).start()

    def after_fourth(self):
        for k in range(2):

            @pl.when(self.away(k))
            def _():
                self.fourth(k).wait_send()

            @pl.when(self.holds(k))
            def _():
                at = self.piece(k)
                mine = self.z_hi * 2 + k
                seven = self.r4.at[pl.ds(0, 7), at]
                self.wait(seven, seven, 4, 4, send=False)
                self.r4[mine, at, :] = self.a3[at, :]
                total = self.r4[0, at, :].astype(F32)
                for z in range(1, 8):
                    total += self.r4[z, at, :].astype(F32)
                self.out[at, :] = total.astype(BF16)
                for s in range(1, R):
                    self.fifth(k, s).start()

    def finish(self):
        for k in range(2):

            @pl.when(self.holds(k))
            def _():
                seven = self.r4.at[pl.ds(0, 7), self.piece(k)]
                self.wait(seven, seven, 6, 5 + k, recv=False)

            @pl.when(self.away(k))
            def _():
                self.fifth(k, 1).wait_recv()

        return self.out[...].astype(F32) * (float(T * NR * R * W) ** -0.5)


def zero_at(ref, where, condition):
    @pl.when(condition)
    def _():
        ref[where] = jnp.zeros(ref[where].shape, ref.dtype)


def block_kernel(
    x_hbm, g_hbm, w_hbm, aw_hbm,
    dx, dconv, dattn,
    xe, ae, hid, w_ref, kt, aw, joined, gpad, gt, mpad, mt, pt, gm,
    xc, ac, ge, uc, pre, pc, g1, xt, at0, at1, xs, as0, as1, u0, s0, u1, s1,
    gs, gr, ms, mr, ps, pr, hs, hr, ks, kr, ls, ts, tr,
    *bufs,
):
    tm, rows = lax.axis_index("tm"), lax.axis_index("rows")
    up = {"rows": lax.rem(rows + R - 1, R)}
    down = {"rows": lax.rem(rows + 1, R)}
    top, bottom = rows == 0, rows == R - 1
    work, bufs = bufs[:10], bufs[10:]
    attn = Reduction(2, 1, False, bufs[:13], tm, rows)
    early = Reduction(4, 2, True, bufs[13:24], tm, rows)
    late = Reduction(5, 3, True, bufs[24:], tm, rows)
    core = lax.rem(tm, 2)
    twin = {"tm": tm + 1 - 2 * core}
    g_bufs, m_bufs, p_bufs = (gpad, gt, gs, gr), (mpad, mt, ms, mr), (pt, gm, ps, pr)

    loads = [
        pltpu.make_async_copy(x_hbm, xe.at[pl.ds(2, NR)], ls.at[0]),
        *(
            pltpu.make_async_copy(
                g_hbm.at[pl.ds(first, count)], gpad.at[half, pl.ds(device, count)], ls.at[1 + k]
            )
            for k, (half, device, first, count) in enumerate(
                ((0, 1, 0, 9), (0, 11, 9, 1), (0, 12, 40, 20), (1, 0, 10, 20), (1, 21, 30, 9), (1, 31, 39, 1))
            )
        ),
        pltpu.make_async_copy(w_hbm, w_ref, ls.at[7]),
        pltpu.make_async_copy(aw_hbm, aw, ls.at[8]),
    ]
    for load in loads:
        load.start()
    for half in range(2):
        for device in IDLE[half]:
            gpad[half, device] = jnp.zeros((PIX, C), BF16)
            mpad[half, device] = jnp.zeros((PIX, C), BF16)
    barrier(tm, rows)
    loads[0].wait()
    to_up = remote(xe.at[pl.ds(2, 2)], xe.at[pl.ds(NR + 2, 2)], hs.at[0], hr.at[0], up)
    to_down = remote(xe.at[pl.ds(NR, 2)], xe.at[pl.ds(0, 2)], hs.at[1], hr.at[1], down)
    to_up.start()
    to_down.start()
    for load in loads[1:7]:
        load.wait()
    spread_start(g_bufs, 0, tm)
    spread_start(g_bufs, 1, tm)
    fill(xe, xc, 2, NR, True)

    def keep(first, hidden):
        hid[first : first + hidden.shape[0]] = hidden
        ae[first : first + hidden.shape[0]] = (hidden * jax.nn.sigmoid(hidden)).astype(BF16)

    loads[7].wait()
    keep(2, conv(xc, ((2, 4),), w_ref[0], True))
    to_up.wait()
    to_down.wait()
    zero_at(xe, slice(0, 2), top)
    zero_at(xe, slice(NR + 2, NR + 4), bottom)
    fill(xe, xc, 0, 2, True)
    fill(xe, xc, NR + 2, 2, True)
    ends = conv(xc, ((0, 2), (6, 2)), w_ref[0], True)
    keep(0, ends[0:2])
    keep(6, ends[2:4])
    zero_at(ae, slice(0, 1), top)
    zero_at(ae, slice(NR + 1, NR + 2), bottom)
    fill(ae, ac, 0, NR + 2, True)
    branch = conv(ac, ((0, 1), (4, 2)), w_ref[1], True)
    mixed = jnp.concatenate([xe[2:3], xe[6:8]], axis=0).astype(F32) + branch
    spread_out(mpad, 0, mixed.astype(BF16).reshape(30, PIX, C))
    spread_start(m_bufs, 0, tm)
    mixed = xe[3:6].astype(F32) + conv(ac, ((1, 3),), w_ref[1], True)
    spread_out(mpad, 1, mixed.astype(BF16).reshape(30, PIX, C))
    spread_wait(g_bufs, 0, tm)
    loads[8].wait()
    joined[...] = jnp.concatenate([aw[0], aw[1], aw[2]], axis=1)

    def turn(i, _):
        for k in range(2):
            at = pl.ds(pl.multiple_of(i * C, C), C)
            kt[k, at, :] = w_ref[k, at, :].astype(F32).T.astype(BF16)
        return 0

    lax.fori_loop(0, 9, turn, 0)

    def slopes(i, _):
        h = hid[i]
        s = jax.nn.sigmoid(h)
        hid[i] = s * (1.0 + h * (1.0 - s))
        return 0

    lax.fori_loop(0, NR + 2, slopes, 0)

    def flip(to, a, b, pieces, depth):
        rows_in = [p.reshape(-1, C).astype(F32) for p in pieces]
        short = depth - sum(p.shape[0] for p in rows_in)
        flat = jnp.concatenate(rows_in + [jnp.zeros((short, C), F32)], axis=0).T
        flat = flat.reshape(16, 2, 8, depth)
        for c in range(2):
            to[c, a, b * 128 : (b + 1) * 128, :] = flat[:, c].reshape(128, depth).astype(BF16)

    def flips(a, _):
        for b in range(3):
            at = pl.ds(b * C, C)
            flip(xt, a, b, [xc[pl.ds(a + 1, NR), :, at]], 1024)
            flip(at0, a, b, [ac[pl.ds(a, 1), :, at], ac[pl.ds(a + 4, 2), :, at]], 512)
            flip(at1, a, b, [ac[pl.ds(a + 1, 3), :, at]], 512)
        return 0

    lax.fori_loop(0, 3, flips, 0)
    swaps = [
        remote(src.at[1 - core], dst, ts.at[k], tr.at[k], twin)
        for k, (src, dst) in enumerate(((at0, as0), (at1, as1), (xt, xs)))
    ]
    for buf in (u1, s1):
        buf[:, 480:512] = jnp.zeros((2, 32, C), BF16)
    for buf in (u0, s0):
        buf[960:1024] = jnp.zeros((64, C), BF16)
    full = pl.ds(0, 480)
    u_swaps = [
        remote(u1.at[0, full], s1.at[0, full], ts.at[3], tr.at[3], twin),
        remote(u1.at[1, full], s1.at[1, full], ts.at[4], tr.at[4], twin),
        remote(u0.at[pl.ds(0, 960)], s0.at[pl.ds(0, 960)], ts.at[5], tr.at[5], twin),
    ]
    spread_wait(g_bufs, 1, tm)
    spread_start(m_bufs, 1, tm)
    for swap in swaps:
        swap.start()
    for half in range(2):
        spread_wait(m_bufs, half, tm)
        attend(half, mt, gt, pt, aw, joined, work, UNROLL)
        spread_start(p_bufs, half, tm, True)

    gup, normed, att, gj = work[6:10]
    proj = tn(normed[...], gj[...])
    attn.send(0, proj[:, 0:C], proj[:, C : 2 * C])
    attn.send(1, proj[:, 2 * C : 3 * C], tn(att[...], gup[...]))

    spread_wait(p_bufs, 0, tm, True)
    outer = gathered(gm, 0)
    ge[2:3] = outer[0:W].reshape(1, W, C)
    ge[6:8] = outer[W:].reshape(2, W, C)
    u1[0, 0:480] = outer
    u_swaps[0].start()
    near_up = remote(ge.at[2], ge.at[NR + 2], ks.at[0], kr.at[0], up)
    near_down = remote(ge.at[NR + 1], ge.at[1], ks.at[1], kr.at[1], down)
    near_up.start()
    near_down.start()
    fill(ge, uc, 2, 1, False)
    fill(ge, uc, 6, 2, False)

    def times(a, b):
        return jnp.dot(a, b, preferred_element_type=F32)

    for swap in swaps:
        swap.wait()
    u_swaps[0].wait()
    for a in range(3):
        g1[a] = times(at0[core, a], u1[0]) + times(as0[a], s1[0])
    attn.after_core()

    def one(k):
        return g1[k // 3, (k % 3) * 128 : (k % 3 + 1) * 128, :]

    spread_wait(p_bufs, 1, tm, True)
    inner = gathered(gm, 1)
    ge[3:6] = inner.reshape(3, W, C)
    u1[1, 0:480] = inner
    u_swaps[1].start()
    far_up = remote(ge.at[3], ge.at[NR + 3], ks.at[2], kr.at[2], up)
    far_down = remote(ge.at[NR], ge.at[0], ks.at[3], kr.at[3], down)
    far_up.start()
    far_down.start()
    fill(ge, uc, 3, 3, False)

    def back(first, act_grad):
        at = slice(first, first + act_grad.shape[0])
        pre[at] = (act_grad.astype(BF16).astype(F32) * hid[at]).astype(BF16)

    near_up.wait()
    near_down.wait()
    zero_at(ge, slice(1, 2), top)
    zero_at(ge, slice(NR + 2, NR + 3), bottom)
    fill(ge, uc, 1, 1, False)
    fill(ge, uc, NR + 2, 1, False)
    back(1, conv(uc, ((1, 6),), kt[1], False))
    u0[0:960] = pre[1 : NR + 1].reshape(960, C)
    u_swaps[2].start()
    u_swaps[1].wait()
    for a in range(3):
        g1[a] += times(at1[core, a], u1[1]) + times(as1[a], s1[1])
        for j in ((0,), (1, 2), (3,))[a]:
            early.send(j, one(2 * j), one(2 * j + 1))
    g0 = []

    def zero(k):
        return g0[k // 3][(k % 3) * 128 : (k % 3 + 1) * 128]

    u_swaps[2].wait()
    for a in range(3):
        g0.append(times(xt[core, a], u0[...]) + times(xs[a], s0[...]))
        for j in ((0,), (1, 2), (3, 4))[a]:
            late.send(j, zero(2 * j), zero(2 * j + 1) if j < 4 else one(8))
    attn.after_second()
    far_up.wait()
    far_down.wait()
    zero_at(ge, slice(0, 1), top)
    zero_at(ge, slice(NR + 3, NR + 4), bottom)
    fill(ge, uc, 0, 1, False)
    fill(ge, uc, NR + 3, 1, False)
    ends = conv(uc, ((0, 1), (7, 1)), kt[1], False)
    back(0, ends[0:1])
    back(7, ends[1:2])
    zero_at(pre, slice(0, 1), top)
    zero_at(pre, slice(NR + 1, NR + 2), bottom)
    fill(pre, pc, 0, NR + 2, False)
    early.after_second()
    dx[...] = (ge[2:8].astype(F32) + conv(pc, ((0, 6),), kt[0], False)).astype(BF16)
    attn.after_third()
    late.after_second()
    early.after_third()
    late.after_third()
    attn.after_fourth()
    early.after_fourth()
    late.after_fourth()
    dattn[...] = attn.finish().reshape(4, 8, C)
    dconv[1, 0:8] = early.finish().reshape(8, 8, C)
    sums = late.finish()
    dconv[0] = sums[0:72].reshape(9, 8, C)
    dconv[1, 8:9] = sums[72:80].reshape(1, 8, C)


def pass_kernel(a, b, c, x, y, z, va, vb, vc, sems):
    trips = [(a.at[i], va.at[i], x.at[i]) for i in range(NR)] + [(b, vb, y), (c, vc, z)]
    into = [pltpu.make_async_copy(s, v, sems.at[k]) for k, (s, v, _) in enumerate(trips)]
    out = [pltpu.make_async_copy(v, d, sems.at[8 + k]) for k, (_, v, d) in enumerate(trips)]
    for copy in into:
        copy.start()
    for k in range(8):
        into[k].wait()
        out[k].start()
    for copy in out:
        copy.wait()


def anywhere(count):
    return [pl.BlockSpec(memory_space=pl.ANY)] * count


def vmem(count):
    return [pl.BlockSpec(memory_space=pltpu.VMEM)] * count


def dma(*shape):
    return pltpu.SemaphoreType.DMA(shape)


def params(collective_id=None):
    if collective_id is None:
        return pltpu.CompilerParams(vmem_limit_bytes=VMEM_LIMIT)
    return pltpu.CompilerParams(
        vmem_limit_bytes=VMEM_LIMIT, collective_id=collective_id, has_side_effects=True
    )


def per_device(frames_in, grad_out, conv_weight, attn_weight):
    x = frames_in.reshape(NR, W, C)
    g = grad_out.reshape(NR * W // PIX, PIX, C)
    w = conv_weight.reshape(2, 9 * C, C)
    spread = pltpu.VMEM((2, T, PIX, C), BF16)
    shapes = [
        jax.ShapeDtypeStruct((NR, W, C), BF16),
        jax.ShapeDtypeStruct((2, 9, 8, C), F32),
        jax.ShapeDtypeStruct((4, 8, C), F32),
    ]
    outs = pl.pallas_call(
        block_kernel,
        out_shape=shapes,
        in_specs=anywhere(4),
        out_specs=vmem(3),
        scratch_shapes=[
            pltpu.VMEM((NR + 4, W, C), BF16),
            pltpu.VMEM((NR + 2, W, C), BF16),
            pltpu.VMEM((NR + 2, W, C), F32),
            pltpu.VMEM((2, 9 * C, C), BF16),
            pltpu.VMEM((2, 9 * C, C), BF16),
            pltpu.VMEM((4, C, C), BF16),
            pltpu.VMEM((C, 3 * C), BF16),
            *[spread] * 6,
            pltpu.VMEM((NR + 4, W, 3 * C), BF16),
            pltpu.VMEM((NR + 2, W, 3 * C), BF16),
            pltpu.VMEM((NR + 4, W, C), BF16),
            pltpu.VMEM((NR + 4, W, 3 * C), BF16),
            pltpu.VMEM((NR + 2, W, C), BF16),
            pltpu.VMEM((NR + 2, W, 3 * C), BF16),
            pltpu.VMEM((3, 384, C), F32),
            pltpu.VMEM((2, 3, 384, 1024), BF16),
            pltpu.VMEM((2, 3, 384, 512), BF16),
            pltpu.VMEM((2, 3, 384, 512), BF16),
            pltpu.VMEM((3, 384, 1024), BF16),
            pltpu.VMEM((3, 384, 512), BF16),
            pltpu.VMEM((3, 384, 512), BF16),
            pltpu.VMEM((1024, C), BF16),
            pltpu.VMEM((1024, C), BF16),
            pltpu.VMEM((2, 512, C), BF16),
            pltpu.VMEM((2, 512, C), BF16),
            *[dma(2)] * 6,
            dma(2), dma(2), dma(4), dma(4), dma(9), dma(6), dma(6),
            *attend_buffers(),
            *Reduction.buffers(2, 1, False),
            *Reduction.buffers(4, 2, True),
            *Reduction.buffers(5, 3, True),
        ],
        compiler_params=params(1),
        name="block",
    )(x, g, w, attn_weight)
    dx, dconv, dattn = pl.pallas_call(
        pass_kernel,
        out_shape=shapes,
        in_specs=anywhere(3),
        out_specs=anywhere(3),
        scratch_shapes=[*[pltpu.VMEM(s.shape, s.dtype) for s in shapes], dma(16)],
        compiler_params=params(),
        name="hand_on",
    )(*outs)
    return dx.reshape(1, NR, W, C), dconv, dattn


def solution(mesh):
    return jax.shard_map(
        per_device,
        mesh=mesh,
        in_specs=(P("tm", "rows", None, None), P("tm", "rows", None, None), P(), P()),
        out_specs=(P("tm", "rows", None, None), P(None, None, "tm", None), P(None, "tm", None)),
        check_vma=False,
    )
```
